128 devices in a mesh: dp: 4 (over y), shard: 32 (over z, x, core).
Axes of the slice: x: 4, y: 4, z: 4, core: 2. Of those that a mesh axis runs over, the one named last changes fastest.
Arguments:
- grads: bfloat16 [4, 64, 1024, 1024], P('dp', None, 'shard'), may hold values from -6 to 6
- params: bfloat16 [64, 1024, 1024], P(None, 'shard'), may hold values from -6 to 6
- stats: float32 [4, 32, 1024, 1024], P('dp', 'shard'), may hold values from -1 to 17, as said below
- roots: float32 [4, 32, 1024, 1024], P('dp', 'shard'), may hold values from -1 to 2, as said below
- table: int32 [4, 16], replicated, may hold values from 0 to 15, each once within a row
Outputs:
- new_params: bfloat16 [64, 1024, 1024], P(None, 'shard')
- new_stats: float32 [4, 32, 1024, 1024], P('dp', 'shard')
The draws below stay inside these ranges and needn't reach their ends.
Inputs may be any that keep to these rules, and one draw needn't show every extreme that they name: Each row of table names each of the 16 blocks of its group once. Every matrix stats[d, s] is symmetric. Every matrix roots[d, s] is symmetric.
All inputs are finite; a program needn't handle non-finite values.
Results may differ from the reference program's by a relative error of at most 0.0085.
Values may be sent and summed in bfloat16 or wider, within the bound.
No kernel may reach another device: no remote copies, remote signals or barrier semaphores. Data moves between devices by JAX's collectives and lax.ppermute only.
A program may use at most 128 MiB of HBM per device.

```python
import math
import jax
import jax.numpy as jnp
from jax import lax

BS = 1024
NB = 64
N_DP = 4
N_SHARD = 32


def draw_stats(key, part):
    key = jax.random.fold_in(key, 11)
    first_key, second_key = jax.random.split(key)
    shape = (N_DP, N_SHARD, BS, BS)
    diagonal = jnp.exp(jax.random.uniform(first_key, (N_DP, N_SHARD, 1, BS), jnp.float32, 0.0, math.log(10.0)))
    noise = jax.random.normal(second_key, shape, jnp.float32)
    noise = noise * (0.25 / math.sqrt(BS))
    symmetric = noise + jnp.swapaxes(noise, -1, -2)
    return symmetric + jnp.eye(BS, dtype=jnp.float32) * diagonal


def draw_roots(key, part):
    key = jax.random.fold_in(key, 23)
    first_key, second_key = jax.random.split(key)
    shape = (N_DP, N_SHARD, BS, BS)
    diagonal = jnp.exp(jax.random.uniform(first_key, (N_DP, N_SHARD, 1, BS), jnp.float32, math.log(0.25), math.log(1.0)))
    noise = jax.random.normal(second_key, shape, jnp.float32)
    noise = noise * (0.1 / math.sqrt(BS))
    symmetric = noise + jnp.swapaxes(noise, -1, -2)
    return symmetric + jnp.eye(BS, dtype=jnp.float32) * diagonal


def with_spikes(array, rng, source, target, shards_of, factor):
    owner, partner = [(jnp.arange(array.shape[position]) // (array.shape[position] // shards_of)).reshape([-1 if axis == position else 1 for axis in range(array.ndim)]) for position in (source, target)]
    chosen = jax.random.permutation(rng, shards_of)[partner]
    strong = (owner == chosen) | (owner == (partner + shards_of // 2) % shards_of)
    return jnp.where(strong, factor * array, array)


def steps_of(own_key, shape, shards, least, high):
    def one(dim, blocks):
        steps = jax.random.uniform(jax.random.fold_in(jax.random.fold_in(own_key, 6), dim), (blocks,), jnp.float32, least / len(shards), high / len(shards))
        return jnp.repeat(jnp.exp(steps), shape[dim] // blocks).reshape((-1,) + (1,) * (len(shape) - dim - 1))

    loudness = one(*shards[0])
    for cut in shards[1:]:
        loudness = loudness * one(*cut)
    return loudness


def centred(key, dims, width, bound, pieces=(), held_as=jnp.bfloat16):
    drawn = jax.random.normal(key, dims, jnp.float32) * width
    if len(pieces) > 0:
        drawn = steps_of(key, dims, pieces, -0.22, 0.18) * drawn
    return jnp.clip(drawn, min=-bound, max=bound).astype(held_as)


def heavy_noise(rng, shape, scale, bound, pieces, heavy, held_as=jnp.bfloat16):
    result = scale * jax.random.normal(rng, shape, jnp.float32)
    if pieces:
        result = result * steps_of(rng, shape, pieces, -0.22, 0.18)
    return jnp.clip(with_spikes(result, jax.random.fold_in(rng, 3), *heavy), -bound, bound).astype(held_as)


def setup_inputs(seed: int = 0) -> dict:
    arg_keys = jax.random.split(jax.random.key(seed), 6)
    grads = heavy_noise(arg_keys[0], (N_DP, NB, BS, BS), 1.0, 6.0, ((0, 4), (2, 32)), (0, 1, 4, 2.0))
    params = centred(arg_keys[1], (NB, BS, BS), 1.0, 6.0, ((1, 32),))
    stats = draw_stats(jax.random.fold_in(arg_keys[5], 71), 0)
    roots = draw_roots(jax.random.fold_in(arg_keys[5], 71), 0)
    table = jax.vmap(lambda own: jax.random.permutation(own, N_SHARD // 2))(jax.random.split(arg_keys[4], N_DP)).reshape((N_DP, N_SHARD // 2)).astype(jnp.int32)
    return dict(grads=grads, params=params, stats=stats, roots=roots, table=table)


keep_rate = 0.75
step_size = 0.25


def reference(grads, params, stats, roots, table):
    summed = jnp.sum(grads.astype(jnp.float32), axis=0).astype(jnp.bfloat16)
    row_blocks = NB // N_DP
    owners = (jnp.arange(N_DP, dtype=jnp.int32)[:, None] * row_blocks + table.astype(jnp.int32)).reshape(-1).astype(jnp.int32)
    pair_stats = stats.reshape(NB, 2, BS, BS)
    pair_roots = roots.reshape(NB, 2, BS, BS)

    def per_pair(item):
        block_id, stat_pair, root_pair = item
        gradient = lax.dynamic_index_in_dim(summed, block_id, 0, keepdims=False)
        left_gram = jnp.dot(gradient, gradient.T, preferred_element_type=jnp.float32)
        right_gram = jnp.dot(gradient.T, gradient, preferred_element_type=jnp.float32)
        new_left = keep_rate * stat_pair[0] + ((1.0 - keep_rate) / BS) * left_gram
        new_right = keep_rate * stat_pair[1] + ((1.0 - keep_rate) / BS) * right_gram
        first = jnp.dot(root_pair[0], gradient.astype(jnp.float32), precision=lax.Precision.HIGHEST)
        update = jnp.dot(first, root_pair[1], precision=lax.Precision.HIGHEST)
        return jnp.stack([new_left, new_right]), update

    new_stats, updates = lax.map(per_pair, (owners, pair_stats, pair_roots))
    ordered = jnp.zeros((NB, BS, BS), jnp.float32).at[owners].set(updates)
    new_params = (params.astype(jnp.float32) - step_size * ordered).astype(jnp.bfloat16)
    return new_params, new_stats.reshape(N_DP, N_SHARD, BS, BS)
```

```python
import jax
import jax.numpy as jnp
from jax import lax
from jax.sharding import PartitionSpec as P

keep_rate = 0.75
step_size = 0.25
f32 = jnp.float32
bf16 = jnp.bfloat16


def shifted(block, axis, offset):
    count = lax.axis_size(axis)
    return lax.ppermute(block, axis, [(i, (i + offset) % count) for i in range(count)])


def other_core(block):
    count = lax.axis_size("shard")
    return lax.ppermute(block, "shard", [(i, i ^ 1) for i in range(count)])


def exchanged(blocks):
    return lax.all_to_all(blocks, "shard", split_axis=0, concat_axis=0, tiled=True)


def picked(array, index):
    return array.at[index].get(mode="promise_in_bounds")


def added(*terms):
    total = terms[0].astype(f32)
    for term in terms[1:]:
        total = total + term.astype(f32)
    return total.astype(bf16)


def in_order(values, after):
    held = lax.optimization_barrier(tuple(values) + tuple(after))
    return held[: len(values)]


def on_device(grads, params, stats, roots, table):
    shards = lax.axis_size("shard")
    replicas = lax.axis_size("dp")
    blocks = grads.shape[1]
    group = blocks // replicas
    rows = grads.shape[2]
    size = grads.shape[3]
    half_rows = rows // 2
    half = group // 2
    replica = lax.axis_index("dp")
    core = lax.axis_index("shard") % 2
    own_order = lax.dynamic_index_in_dim(table, replica, 0, keepdims=False)
    places = jnp.arange(group, dtype=table.dtype)
    own_inverse = jnp.sum(
        jnp.where(own_order[None, :] == places[:, None], places[None, :], 0), axis=1
    )
    mine = grads[0]

    def piece(step, which):
        start = (replica + step) % replicas * group + which * half
        return lax.dynamic_slice_in_dim(mine, start, half, 0)

    far = (piece(2, 0), piece(2, 1))
    near = in_order((piece(1, 1), piece(3, 0)), far)
    far_up = shifted(far[0], "dp", 1)
    far_down = shifted(far[1], "dp", -1)
    near_up = shifted(near[0], "dp", 1)
    near_down = shifted(near[1], "dp", -1)

    root = in_order((roots[0, 0],), near)[0].astype(bf16)
    partner_root = other_core(root)
    tall = (shards, 2, half_rows, size)
    left_rows = jnp.where(
        core == 0, root.reshape(tall)[:, 0], partner_root.reshape(tall)[:, 1]
    ).reshape(size // 2, size)
    right = jnp.where(core == 0, partner_root, root)

    sums = (added(piece(1, 0), far_up), added(piece(3, 1), far_down))
    sum_up = shifted(sums[0], "dp", 1)
    sum_down = shifted(sums[1], "dp", -1)
    low = added(piece(0, 0), near_down, sum_up)
    high = added(piece(0, 1), near_up, sum_down)
    whole = picked(jnp.concatenate([low, high]), own_order)
    whole, left_rows, right = lax.optimization_barrier((whole, left_rows, right))

    own_rows = exchanged(whole.reshape(shards, half_rows, size))
    other_rows = other_core(own_rows)
    gradient = jnp.zeros((shards, 2, half_rows, size), bf16)
    gradient = lax.dynamic_update_slice(gradient, own_rows[:, None], (0, core, 0, 0))
    gradient = lax.dynamic_update_slice(gradient, other_rows[:, None], (0, 1 - core, 0, 0))
    gradient = gradient.reshape(size, size)
    first = jnp.dot(left_rows, gradient, preferred_element_type=f32).astype(bf16)
    update = jnp.dot(first, right, preferred_element_type=f32).astype(bf16)
    update = exchanged(update.reshape(shards, half_rows, size))

    oriented = jnp.where(core == 0, gradient, gradient.T)
    outer_product = jnp.dot(oriented, oriented.T, preferred_element_type=f32)
    new_stat = keep_rate * stats[0, 0] + (1.0 - keep_rate) / size * outer_product
    out = jnp.zeros(params.shape, bf16)
    update, new_stat, out = lax.optimization_barrier((update, new_stat, out))

    update = update.reshape(group, rows, size)
    own_params = lax.dynamic_slice_in_dim(params, replica * group, group, 0)

    def fresh(which):
        these = slice(which * half, (which + 1) * half)
        moved = picked(update, own_inverse[these]).astype(f32)
        return (own_params[these].astype(f32) - step_size * moved).astype(bf16)

    def placed(out, block, step, which):
        start = (replica + step) % replicas * group + which * half
        return lax.dynamic_update_slice_in_dim(out, block, start, 0)

    low, high = fresh(0), fresh(1)
    low_below = shifted(low, "dp", 1)
    high_above = shifted(high, "dp", -1)
    high_below = shifted(high, "dp", 1)
    low_above = shifted(low, "dp", -1)
    low_far = shifted(low_below, "dp", 1)
    high_far = shifted(high_above, "dp", -1)
    out = placed(out, low, 0, 0)
    out = placed(out, high, 0, 1)
    out = placed(out, low_below, 3, 0)
    out = placed(out, high_above, 1, 1)
    out = placed(out, high_below, 3, 1)
    out = placed(out, low_above, 1, 0)
    out = placed(out, low_far, 2, 0)
    out = placed(out, high_far, 2, 1)
    return (out, new_stat[None, None])


def solution(mesh):
    placed = (
        P("dp", None, "shard", None),
        P(None, "shard", None),
        P("dp", "shard", None, None),
        P("dp", "shard", None, None),
        P(),
    )
    return jax.shard_map(
        on_device,
        mesh=mesh,
        in_specs=placed,
        out_specs=(P(None, "shard", None), P("dp", "shard", None, None)),
        check_vma=False,
    )
```

```python
import functools

import jax
import jax.numpy as jnp
from jax import lax
from jax.experimental import pallas as pl
from jax.experimental.pallas import tpu as pltpu
from jax.sharding import PartitionSpec as P

keep_rate = 0.75
step_size = 0.25
f32 = jnp.float32
bf16 = jnp.bfloat16


def shifted(block, axis, offset):
    count = lax.axis_size(axis)
    return lax.ppermute(block, axis, [(i, (i + offset) % count) for i in range(count)])


def other_core(block):
    count = lax.axis_size("shard")
    return lax.ppermute(block, "shard", [(i, i ^ 1) for i in range(count)])


def exchanged(blocks):
    return lax.all_to_all(blocks, "shard", split_axis=0, concat_axis=0, tiled=True)


def added(*terms):
    total = terms[0].astype(f32)
    for term in terms[1:]:
        total = total + term.astype(f32)
    return total.astype(bf16)


def in_order(values, after):
    held = lax.optimization_barrier(tuple(values) + tuple(after))
    return held[: len(values)]


def whole_in(space):
    return pl.BlockSpec(memory_space=space)


def finish_sum_kernel(order, low, high, sum_low, sum_high, out):
    half = low.shape[0]

    def step(place, carry):
        block = order[place]

        @pl.when(block < half)
        def _():
            out[place] = added(low[block], sum_low[block])

        @pl.when(block >= half)
        def _():
            out[place] = added(high[block - half], sum_high[block - half])

        return carry

    lax.fori_loop(0, out.shape[0], step, 0)


def finish_sum(order, *terms):
    shape = (order.shape[0],) + terms[0].shape[1:]
    size = terms[0].size * 2
    return pl.pallas_call(
        finish_sum_kernel,
        out_shape=jax.ShapeDtypeStruct(shape, bf16),
        in_specs=[whole_in(pltpu.SMEM)] + [whole_in(pltpu.VMEM)] * 4,
        out_specs=whole_in(pltpu.VMEM),
        compiler_params=pltpu.CompilerParams(vmem_limit_bytes=16 << 20),
        cost_estimate=pl.CostEstimate(flops=size, bytes_accessed=6 * size, transcendentals=0),
        name="finish_sum",
    )(order, *terms)


def interleaved(core, own, other, gradient):
    half_rows = own.shape[1]

    def place(shard, carry):
        start = shard * 2 * half_rows
        here = pl.multiple_of(start + core * half_rows, half_rows)
        there = pl.multiple_of(start + (1 - core) * half_rows, half_rows)
        gradient[pl.ds(here, half_rows), :] = own[shard]
        gradient[pl.ds(there, half_rows), :] = other[shard]
        return carry

    lax.fori_loop(0, own.shape[0], place, 0, unroll=4)


def orient_kernel(core, root, partner, left, right, rows, moved):
    shards, _, half_rows, size = root.shape
    half = size // 2

    def rows_of(shard):
        return pl.ds(pl.multiple_of(shard * half_rows, half_rows), half_rows)

    def place_from(source, which):
        def place(shard, carry):
            rows[rows_of(shard), :] = source[shard, which]
            return carry

        lax.fori_loop(0, shards, place, 0)

    @pl.when(core[0] == 0)
    def _():
        right[...] = partner[...].reshape(size, size)
        place_from(root, 0)

    @pl.when(core[0] == 1)
    def _():
        right[...] = root[...].reshape(size, size)
        place_from(partner, 1)

    for side in range(2):
        place = lax.broadcasted_iota(jnp.int32, (size, half), 1)
        which = core[0] if side == 0 else 1 - core[0]
        source = 2 * half_rows * (place // half_rows) + which * half_rows + place % half_rows
        chosen = lax.broadcasted_iota(jnp.int32, (size, half), 0) == source
        moved[...] = jnp.where(chosen, 1.0, 0.0).astype(bf16)
        left[side] = jnp.dot(rows[...], moved[...], preferred_element_type=f32).astype(bf16)


def oriented(core, root, partner):
    shards, _, half_rows, size = root.shape
    half = size // 2
    return pl.pallas_call(
        orient_kernel,
        out_shape=[
            jax.ShapeDtypeStruct((2, half, half), bf16),
            jax.ShapeDtypeStruct((size, size), bf16),
        ],
        in_specs=[whole_in(pltpu.SMEM)] + [whole_in(pltpu.VMEM)] * 2,
        out_specs=[whole_in(pltpu.VMEM)] * 2,
        scratch_shapes=[pltpu.VMEM((half, size), bf16), pltpu.VMEM((size, half), bf16)],
        compiler_params=pltpu.CompilerParams(vmem_limit_bytes=24 << 20),
        cost_estimate=pl.CostEstimate(flops=size**3, bytes_accessed=12 * size**2, transcendentals=0),
        name="orient",
    )(core, root, partner)


def begin_kernel(left, rows, part):
    half, size = part.shape
    width = size // 4
    for low in range(0, size, width):
        columns = slice(low, low + width)
        part[:, columns] = jnp.dot(
            left[0], rows[:, :, columns].reshape(half, width), preferred_element_type=f32
        )


def begun(left, rows):
    half, size = left.shape[1], rows.shape[2]
    return pl.pallas_call(
        begin_kernel,
        out_shape=jax.ShapeDtypeStruct((half, size), f32),
        in_specs=[whole_in(pltpu.VMEM)] * 2,
        out_specs=whole_in(pltpu.VMEM),
        compiler_params=pltpu.CompilerParams(vmem_limit_bytes=16 << 20),
        cost_estimate=pl.CostEstimate(flops=size**3 // 2, bytes_accessed=4 * size**2, transcendentals=0),
        name="begin",
    )(left, rows)


def complete_kernel(part, left, rows, right, update, first):
    half, size = part.shape
    width = size // 4
    for low in range(0, size, width):
        columns = slice(low, low + width)
        product = jnp.dot(
            left[1], rows[:, :, columns].reshape(half, width), preferred_element_type=f32
        )
        first[:, columns] = (part[:, columns] + product).astype(bf16)
    for low in range(0, size, width):
        columns = slice(low, low + width)
        update[:, columns] = jnp.dot(
            first[...], right[:, columns], preferred_element_type=f32
        ).astype(bf16)


def completed(part, left, rows, right):
    half, size = part.shape
    return pl.pallas_call(
        complete_kernel,
        out_shape=jax.ShapeDtypeStruct((half, size), bf16),
        in_specs=[whole_in(pltpu.VMEM)] * 4,
        out_specs=whole_in(pltpu.VMEM),
        scratch_shapes=[pltpu.VMEM((half, size), bf16)],
        compiler_params=pltpu.CompilerParams(vmem_limit_bytes=24 << 20),
        cost_estimate=pl.CostEstimate(flops=2 * size**3, bytes_accessed=7 * size**2, transcendentals=0),
        name="complete",
    )(part, left, rows, right)


def statistics_kernel(core, own, other, stat, out, gradient):
    size = gradient.shape[0]
    tile = stat.shape[0]
    step = pl.program_id(0)
    mine = core[0]

    @pl.when(step == 0)
    def _():
        interleaved(mine, own, other, gradient)

    rows = pl.ds(pl.multiple_of(step * tile, tile), tile)

    @pl.when(mine == 0)
    def _():
        outer = lax.dot_general(
            gradient[rows, :], gradient[...], (((1,), (1,)), ((), ())), preferred_element_type=f32
        )
        out[...] = keep_rate * stat[...] + (1.0 - keep_rate) / size * outer

    @pl.when(mine == 1)
    def _():
        outer = lax.dot_general(
            gradient[:, rows], gradient[...], (((0,), (0,)), ((), ())), preferred_element_type=f32
        )
        out[...] = keep_rate * stat[...] + (1.0 - keep_rate) / size * outer


def statistics(core, own, other, stat):
    size = stat.shape[0]
    tile = size // 4
    block = pl.BlockSpec((tile, size), lambda step: (step, 0))
    return pl.pallas_call(
        statistics_kernel,
        grid=(size // tile,),
        out_shape=jax.ShapeDtypeStruct(stat.shape, f32),
        in_specs=[whole_in(pltpu.SMEM)] + [whole_in(pltpu.VMEM)] * 2 + [block],
        out_specs=block,
        scratch_shapes=[pltpu.VMEM((size, size), bf16)],
        compiler_params=pltpu.CompilerParams(vmem_limit_bytes=16 << 20),
        cost_estimate=pl.CostEstimate(flops=2 * size**3, bytes_accessed=12 * size**2, transcendentals=0),
        name="statistics",
    )(core, own, other, stat)


def step_kernel(order, old, update, low, high):
    half = low.shape[0]

    def step(place, carry):
        block = order[place]
        fresh = old[block].astype(f32) - step_size * update[place].astype(f32)

        @pl.when(block < half)
        def _():
            low[block] = fresh.astype(bf16)

        @pl.when(block >= half)
        def _():
            high[block - half] = fresh.astype(bf16)

        return carry

    lax.fori_loop(0, old.shape[0], step, 0)


def stepped(order, old, update):
    shape = (old.shape[0] // 2,) + old.shape[1:]
    return pl.pallas_call(
        step_kernel,
        out_shape=[jax.ShapeDtypeStruct(shape, bf16)] * 2,
        in_specs=[whole_in(pltpu.SMEM)] + [whole_in(pltpu.VMEM)] * 2,
        out_specs=[whole_in(pltpu.VMEM)] * 2,
        compiler_params=pltpu.CompilerParams(vmem_limit_bytes=16 << 20),
        cost_estimate=pl.CostEstimate(flops=2 * old.size, bytes_accessed=6 * old.size, transcendentals=0),
        name="step",
    )(order, old, update)


def settle_kernel(replica, low_far, high_far, below, out, sems):
    half = low_far.shape[0]
    replicas = out.shape[0] // (2 * half)
    start = lax.rem(replica[0] + 2, replicas) * 2 * half
    copies = [
        pltpu.make_async_copy(piece, out.at[pl.ds(start + which * half, half)], sems.at[which])
        for which, piece in enumerate((low_far, high_far))
    ]
    for copy in copies:
        copy.start()
    for copy in copies:
        copy.wait()


def settled(replica, low_far, high_far, below):
    return pl.pallas_call(
        settle_kernel,
        out_shape=jax.ShapeDtypeStruct(below.shape, bf16),
        in_specs=[whole_in(pltpu.SMEM)] + [whole_in(pltpu.VMEM)] * 2 + [whole_in(pltpu.HBM)],
        out_specs=whole_in(pltpu.HBM),
        scratch_shapes=[pltpu.SemaphoreType.DMA((2,))],
        input_output_aliases={3: 0},
        compiler_params=pltpu.CompilerParams(vmem_limit_bytes=16 << 20),
        cost_estimate=pl.CostEstimate(flops=0, bytes_accessed=8 * low_far.size, transcendentals=0),
        name="settle",
    )(replica, low_far, high_far, below)


def on_device(grads, params, stats, roots, table):
    shards = lax.axis_size("shard")
    replicas = lax.axis_size("dp")
    blocks = grads.shape[1]
    group = blocks // replicas
    rows = grads.shape[2]
    size = grads.shape[3]
    half_rows = rows // 2
    half = group // 2
    replica = lax.axis_index("dp")
    core = (lax.axis_index("shard") % 2)[None]
    own_order = lax.dynamic_index_in_dim(table, replica, 0, keepdims=False)

    def piece(array, step, which):
        start = (replica + step) % replicas * group + which * half
        return lax.dynamic_slice_in_dim(array, start, half, 0)

    mine = grads[0]
    far = lax.optimization_barrier((piece(mine, 2, 0), piece(mine, 2, 1)))
    far_up = shifted(far[0], "dp", 1)
    far_down = shifted(far[1], "dp", -1)

    root = in_order((roots[0, 0],), far)[0].astype(bf16).reshape(shards, 2, half_rows, size)
    partner_root = other_core(root)
    mine = in_order((mine,), (partner_root,))[0]
    near = lax.optimization_barrier((piece(mine, 1, 1), piece(mine, 3, 0)))
    near_up = shifted(near[0], "dp", 1)
    near_down = shifted(near[1], "dp", -1)

    sums = lax.optimization_barrier(
        (added(piece(mine, 1, 0), far_up), added(piece(mine, 3, 1), far_down))
    )
    sum_up = shifted(sums[0], "dp", 1)
    sum_down = shifted(sums[1], "dp", -1)
    own, near_up, near_down = lax.optimization_barrier(
        (lax.dynamic_slice_in_dim(mine, replica * group, group, 0), near_up, near_down)
    )
    partial = lax.optimization_barrier((added(own[:half], near_down), added(own[half:], near_up)))
    whole = finish_sum(own_order, *partial, sum_up, sum_down)

    own_rows = exchanged(whole.reshape(shards, half_rows, size))
    root, partner_root = in_order((root, partner_root), (whole,))
    left, right = oriented(core, root, partner_root)
    own_rows, left, right = lax.optimization_barrier((own_rows, left, right))
    other_rows = other_core(own_rows)
    part = begun(left, own_rows)
    update = completed(part, left, other_rows, right)

    update = exchanged(update.reshape(shards, half_rows, size))
    new_stat = statistics(core, own_rows, other_rows, stats[0, 0])
    own_params = lax.dynamic_slice_in_dim(params, replica * group, group, 0)
    update, new_stat, own_params = lax.optimization_barrier((update, new_stat, own_params))
    low, high = stepped(own_order, own_params, update.reshape(group, rows, size))
    low_below = shifted(low, "dp", 1)
    high_above = shifted(high, "dp", -1)
    high_below = shifted(high, "dp", 1)
    low_above = shifted(low, "dp", -1)
    low_far = shifted(low_below, "dp", 1)
    high_far = shifted(high_above, "dp", -1)

    def placed(out, block, step, which):
        start = (replica + step) % replicas * group + which * half
        return lax.dynamic_update_slice_in_dim(out, block, start, 0)

    out = jnp.zeros(params.shape, bf16)
    out = placed(out, low_below, 3, 0)
    out = placed(out, high_above, 1, 1)
    out = placed(out, low, 0, 0)
    out = placed(out, high, 0, 1)
    out = placed(out, high_below, 3, 1)
    out = placed(out, low_above, 1, 0)
    out = settled(replica[None], low_far, high_far, out)
    return (out, new_stat[None, None])


def solution(mesh):
    placed = (
        P("dp", None, "shard", None),
        P(None, "shard", None),
        P("dp", "shard", None, None),
        P("dp", "shard", None, None),
        P(),
    )
    return jax.shard_map(
        on_device,
        mesh=mesh,
        in_specs=placed,
        out_specs=(P(None, "shard", None), P("dp", "shard", None, None)),
        check_vma=False,
    )
```

```python
import functools

import jax
import jax.numpy as jnp
from jax import lax
from jax.experimental import pallas as pl
from jax.experimental.pallas import tpu as pltpu
from jax.sharding import PartitionSpec as P

keep_rate = 0.75
step_size = 0.25
f32 = jnp.float32
bf16 = jnp.bfloat16


def shifted(block, axis, offset):
    count = lax.axis_size(axis)
    return lax.ppermute(block, axis, [(i, (i + offset) % count) for i in range(count)])


def other_core(block):
    count = lax.axis_size("shard")
    return lax.ppermute(block, "shard", [(i, i ^ 1) for i in range(count)])


def exchanged(blocks):
    return lax.all_to_all(blocks, "shard", split_axis=0, concat_axis=0, tiled=True)


def added(*terms):
    total = terms[0].astype(f32)
    for term in terms[1:]:
        total = total + term.astype(f32)
    return total.astype(bf16)


def in_order(values, after):
    held = lax.optimization_barrier(tuple(values) + tuple(after))
    return held[: len(values)]


def whole_in(space):
    return pl.BlockSpec(memory_space=space)


def finish_sum_kernel(order, low, high, sum_low, sum_high, out):
    half = low.shape[0]

    def step(place, carry):
        block = order[place]

        @pl.when(block < half)
        def _():
            out[place] = added(low[block], sum_low[block])

        @pl.when(block >= half)
        def _():
            out[place] = added(high[block - half], sum_high[block - half])

        return carry

    lax.fori_loop(0, out.shape[0], step, 0)


def finish_sum(order, *terms):
    shape = (order.shape[0],) + terms[0].shape[1:]
    size = terms[0].size * 2
    return pl.pallas_call(
        finish_sum_kernel,
        out_shape=jax.ShapeDtypeStruct(shape, bf16),
        in_specs=[whole_in(pltpu.SMEM)] + [whole_in(pltpu.VMEM)] * 4,
        out_specs=whole_in(pltpu.VMEM),
        compiler_params=pltpu.CompilerParams(vmem_limit_bytes=16 << 20),
        cost_estimate=pl.CostEstimate(flops=size, bytes_accessed=6 * size, transcendentals=0),
        name="finish_sum",
    )(order, *terms)


def interleaved(core, own, other, gradient):
    half_rows = own.shape[1]

    def place(shard, carry):
        start = shard * 2 * half_rows
        here = pl.multiple_of(start + core * half_rows, half_rows)
        there = pl.multiple_of(start + (1 - core) * half_rows, half_rows)
        gradient[pl.ds(here, half_rows), :] = own[shard]
        gradient[pl.ds(there, half_rows), :] = other[shard]
        return carry

    lax.fori_loop(0, own.shape[0], place, 0, unroll=4)


def orient_kernel(core, root, partner, left, right, left_in, right_in, moved, sems):
    shards, half_rows, size = left_in.shape
    half = size // 2

    def left_copy(source, which):
        return pltpu.make_async_copy(source.at[:, which], left_in, sems.at[0])

    def right_copy(source):
        return pltpu.make_async_copy(source, right_in, sems.at[1])

    @pl.when(core[0] == 0)
    def _():
        left_copy(root, 0).start()
        right_copy(partner).start()

    @pl.when(core[0] == 1)
    def _():
        left_copy(partner, 1).start()
        right_copy(root).start()

    left_copy(root, 0).wait()
    rows = left_in[...].reshape(half, size).astype(bf16)
    for side in range(2):
        place = lax.broadcasted_iota(jnp.int32, (size, half), 1)
        which = core[0] if side == 0 else 1 - core[0]
        source = 2 * half_rows * (place // half_rows) + which * half_rows + place % half_rows
        chosen = lax.broadcasted_iota(jnp.int32, (size, half), 0) == source
        moved[...] = jnp.where(chosen, 1.0, 0.0).astype(bf16)
        left[side] = jnp.dot(rows, moved[...], preferred_element_type=f32).astype(bf16)
    right_copy(root).wait()
    right[...] = right_in[...].reshape(size, size).astype(bf16)


def oriented(core, root, partner):
    shards, _, half_rows, size = root.shape
    half = size // 2
    return pl.pallas_call(
        orient_kernel,
        out_shape=[
            jax.ShapeDtypeStruct((2, half, half), bf16),
            jax.ShapeDtypeStruct((size, size), bf16),
        ],
        in_specs=[whole_in(pltpu.SMEM)] + [whole_in(pl.ANY)] * 2,
        out_specs=[whole_in(pltpu.VMEM)] * 2,
        scratch_shapes=[
            pltpu.VMEM((shards, half_rows, size), f32),
            pltpu.VMEM(root.shape, f32),
            pltpu.VMEM((size, half), bf16),
            pltpu.SemaphoreType.DMA((2,)),
        ],
        compiler_params=pltpu.CompilerParams(vmem_limit_bytes=24 << 20),
        cost_estimate=pl.CostEstimate(flops=size**3, bytes_accessed=12 * size**2, transcendentals=0),
        name="orient",
    )(core, root, partner)


def begin_kernel(left, rows, part):
    half, size = part.shape
    width = size // 4
    for low in range(0, size, width):
        columns = slice(low, low + width)
        part[:, columns] = jnp.dot(
            left[0], rows[:, :, columns].reshape(half, width), preferred_element_type=f32
        )


def begun(left, rows):
    half, size = left.shape[1], rows.shape[2]
    return pl.pallas_call(
        begin_kernel,
        out_shape=jax.ShapeDtypeStruct((half, size), f32),
        in_specs=[whole_in(pltpu.VMEM)] * 2,
        out_specs=whole_in(pltpu.VMEM),
        compiler_params=pltpu.CompilerParams(vmem_limit_bytes=16 << 20),
        cost_estimate=pl.CostEstimate(flops=size**3 // 2, bytes_accessed=4 * size**2, transcendentals=0),
        name="begin",
    )(left, rows)


def complete_kernel(part, left, rows, right_in, update, first, right, arrived):
    half, size = part.shape
    width = size // 4
    fetch = pltpu.make_async_copy(right_in, right, arrived)
    fetch.start()
    for low in range(0, size, width):
        columns = slice(low, low + width)
        product = jnp.dot(
            left[1], rows[:, :, columns].reshape(half, width), preferred_element_type=f32
        )
        first[:, columns] = (part[:, columns] + product).astype(bf16)
    fetch.wait()
    for low in range(0, size, width):
        columns = slice(low, low + width)
        update[:, columns] = jnp.dot(
            first[...], right[:, columns], preferred_element_type=f32
        ).astype(bf16)


def completed(part, left, rows, right):
    half, size = part.shape
    return pl.pallas_call(
        complete_kernel,
        out_shape=jax.ShapeDtypeStruct((half, size), bf16),
        in_specs=[whole_in(pltpu.VMEM)] * 3 + [whole_in(pl.ANY)],
        out_specs=whole_in(pltpu.VMEM),
        scratch_shapes=[
            pltpu.VMEM((half, size), bf16),
            pltpu.VMEM((size, size), bf16),
            pltpu.SemaphoreType.DMA(()),
        ],
        compiler_params=pltpu.CompilerParams(vmem_limit_bytes=24 << 20),
        cost_estimate=pl.CostEstimate(flops=2 * size**3, bytes_accessed=7 * size**2, transcendentals=0),
        name="complete",
    )(part, left, rows, right)


def statistics_kernel(core, own, other, stat, out, gradient):
    size = gradient.shape[0]
    tile = stat.shape[0]
    step = pl.program_id(0)
    mine = core[0]

    @pl.when(step == 0)
    def _():
        interleaved(mine, own, other, gradient)

    rows = pl.ds(pl.multiple_of(step * tile, tile), tile)

    @pl.when(mine == 0)
    def _():
        outer = lax.dot_general(
            gradient[rows, :], gradient[...], (((1,), (1,)), ((), ())), preferred_element_type=f32
        )
        out[...] = keep_rate * stat[...] + (1.0 - keep_rate) / size * outer

    @pl.when(mine == 1)
    def _():
        outer = lax.dot_general(
            gradient[:, rows], gradient[...], (((0,), (0,)), ((), ())), preferred_element_type=f32
        )
        out[...] = keep_rate * stat[...] + (1.0 - keep_rate) / size * outer


def statistics(core, own, other, stat):
    size = stat.shape[0]
    tile = size // 4
    block = pl.BlockSpec((tile, size), lambda step: (step, 0))
    return pl.pallas_call(
        statistics_kernel,
        grid=(size // tile,),
        out_shape=jax.ShapeDtypeStruct(stat.shape, f32),
        in_specs=[whole_in(pltpu.SMEM)] + [whole_in(pltpu.VMEM)] * 2 + [block],
        out_specs=block,
        scratch_shapes=[pltpu.VMEM((size, size), bf16)],
        compiler_params=pltpu.CompilerParams(vmem_limit_bytes=16 << 20),
        cost_estimate=pl.CostEstimate(flops=2 * size**3, bytes_accessed=12 * size**2, transcendentals=0),
        name="statistics",
    )(core, own, other, stat)


def step_kernel(order, old, update, low, high):
    half = low.shape[0]

    def step(place, carry):
        block = order[place]
        fresh = old[block].astype(f32) - step_size * update[place].astype(f32)

        @pl.when(block < half)
        def _():
            low[block] = fresh.astype(bf16)

        @pl.when(block >= half)
        def _():
            high[block - half] = fresh.astype(bf16)

        return carry

    lax.fori_loop(0, old.shape[0], step, 0)


def stepped(order, old, update):
    shape = (old.shape[0] // 2,) + old.shape[1:]
    return pl.pallas_call(
        step_kernel,
        out_shape=[jax.ShapeDtypeStruct(shape, bf16)] * 2,
        in_specs=[whole_in(pltpu.SMEM)] + [whole_in(pltpu.VMEM)] * 2,
        out_specs=[whole_in(pltpu.VMEM)] * 2,
        compiler_params=pltpu.CompilerParams(vmem_limit_bytes=16 << 20),
        cost_estimate=pl.CostEstimate(flops=2 * old.size, bytes_accessed=6 * old.size, transcendentals=0),
        name="step",
    )(order, old, update)


def settle_kernel(replica, low_far, high_far, below, out, sems):
    half = low_far.shape[0]
    replicas = out.shape[0] // (2 * half)
    start = lax.rem(replica[0] + 2, replicas) * 2 * half
    copies = [
        pltpu.make_async_copy(piece, out.at[pl.ds(start + which * half, half)], sems.at[which])
        for which, piece in enumerate((low_far, high_far))
    ]
    for copy in copies:
        copy.start()
    for copy in copies:
        copy.wait()


def settled(replica, low_far, high_far, below):
    return pl.pallas_call(
        settle_kernel,
        out_shape=jax.ShapeDtypeStruct(below.shape, bf16),
        in_specs=[whole_in(pltpu.SMEM)] + [whole_in(pltpu.VMEM)] * 2 + [whole_in(pltpu.HBM)],
        out_specs=whole_in(pltpu.HBM),
        scratch_shapes=[pltpu.SemaphoreType.DMA((2,))],
        input_output_aliases={3: 0},
        compiler_params=pltpu.CompilerParams(vmem_limit_bytes=16 << 20),
        cost_estimate=pl.CostEstimate(flops=0, bytes_accessed=8 * low_far.size, transcendentals=0),
        name="settle",
    )(replica, low_far, high_far, below)


def on_device(grads, params, stats, roots, table):
    shards = lax.axis_size("shard")
    replicas = lax.axis_size("dp")
    blocks = grads.shape[1]
    group = blocks // replicas
    rows = grads.shape[2]
    size = grads.shape[3]
    half_rows = rows // 2
    half = group // 2
    replica = lax.axis_index("dp")
    core = (lax.axis_index("shard") % 2)[None]
    own_order = lax.dynamic_index_in_dim(table, replica, 0, keepdims=False)

    def piece(array, step, which):
        start = (replica + step) % replicas * group + which * half
        return lax.dynamic_slice_in_dim(array, start, half, 0)

    mine = grads[0]
    far = lax.optimization_barrier((piece(mine, 2, 0), piece(mine, 2, 1)))
    far_up = shifted(far[0], "dp", 1)
    far_down = shifted(far[1], "dp", -1)

    root = in_order((roots[0, 0],), far)[0].reshape(shards, 2, half_rows, size)
    partner_root = other_core(root)
    mine = in_order((mine,), (partner_root,))[0]
    near = lax.optimization_barrier((piece(mine, 1, 1), piece(mine, 3, 0)))
    near_up = shifted(near[0], "dp", 1)
    near_down = shifted(near[1], "dp", -1)

    sums = lax.optimization_barrier(
        (added(piece(mine, 1, 0), far_up), added(piece(mine, 3, 1), far_down))
    )
    sum_up = shifted(sums[0], "dp", 1)
    sum_down = shifted(sums[1], "dp", -1)
    own, near_up, near_down = lax.optimization_barrier(
        (lax.dynamic_slice_in_dim(mine, replica * group, group, 0), near_up, near_down)
    )
    partial = lax.optimization_barrier((added(own[:half], near_down), added(own[half:], near_up)))
    whole = finish_sum(own_order, *partial, sum_up, sum_down)

    own_rows = exchanged(whole.reshape(shards, half_rows, size))
    root, partner_root = in_order((root, partner_root), (whole,))
    left, right = oriented(core, root, partner_root)
    own_rows, left, right = lax.optimization_barrier((own_rows, left, right))
    other_rows = other_core(own_rows)
    part = begun(left, own_rows)
    update = completed(part, left, other_rows, right)

    update = exchanged(update.reshape(shards, half_rows, size))
    new_stat = statistics(core, own_rows, other_rows, stats[0, 0])
    own_params = lax.dynamic_slice_in_dim(params, replica * group, group, 0)
    update, new_stat, own_params = lax.optimization_barrier((update, new_stat, own_params))
    low, high = stepped(own_order, own_params, update.reshape(group, rows, size))
    low_below = shifted(low, "dp", 1)
    high_above = shifted(high, "dp", -1)
    high_below = shifted(high, "dp", 1)
    low_above = shifted(low, "dp", -1)
    low_far = shifted(low_below, "dp", 1)
    high_far = shifted(high_above, "dp", -1)

    def placed(out, block, step, which):
        start = (replica + step) % replicas * group + which * half
        return lax.dynamic_update_slice_in_dim(out, block, start, 0)

    out = jnp.zeros(params.shape, bf16)
    out = placed(out, low_below, 3, 0)
    out = placed(out, high_above, 1, 1)
    out = placed(out, low, 0, 0)
    out = placed(out, high, 0, 1)
    out = placed(out, high_below, 3, 1)
    out = placed(out, low_above, 1, 0)
    out = settled(replica[None], low_far, high_far, out)
    return (out, new_stat[None, None])


def solution(mesh):
    placed = (
        P("dp", None, "shard", None),
        P(None, "shard", None),
        P("dp", "shard", None, None),
        P("dp", "shard", None, None),
        P(),
    )
    return jax.shard_map(
        on_device,
        mesh=mesh,
        in_specs=placed,
        out_specs=(P(None, "shard", None), P("dp", "shard", None, None)),
        check_vma=False,
    )
```

```python
import functools

import jax
import jax.numpy as jnp
from jax import lax
from jax.experimental import pallas as pl
from jax.experimental.pallas import tpu as pltpu
from jax.sharding import PartitionSpec as P

keep_rate = 0.75
step_size = 0.25
f32 = jnp.float32
bf16 = jnp.bfloat16


def shifted(block, axis, offset):
    count = lax.axis_size(axis)
    return lax.ppermute(block, axis, [(i, (i + offset) % count) for i in range(count)])


def other_core(block):
    count = lax.axis_size("shard")
    return lax.ppermute(block, "shard", [(i, i ^ 1) for i in range(count)])


def exchanged(blocks):
    return lax.all_to_all(blocks, "shard", split_axis=0, concat_axis=0, tiled=True)


def added(*terms):
    total = terms[0].astype(f32)
    for term in terms[1:]:
        total = total + term.astype(f32)
    return total.astype(bf16)


def in_order(values, after):
    held = lax.optimization_barrier(tuple(values) + tuple(after))
    return held[: len(values)]


def whole_in(space):
    return pl.BlockSpec(memory_space=space)


def finish_sum_kernel(order, low, high, sum_low, sum_high, out, made, sems):
    half = low.shape[0]
    columns = out.shape[3]

    def sent(place, side):
        source = made.at[place, :, pl.ds(side * columns, columns)]
        return pltpu.make_async_copy(source, out.at[place, side], sems.at[side])

    def step(place, carry):
        block = order[place]

        @pl.when(block < half)
        def _():
            made[place] = added(low[block], sum_low[block])

        @pl.when(block >= half)
        def _():
            made[place] = added(high[block - half], sum_high[block - half])

        for side in range(2):
            sent(place, side).start()
        return carry

    def finish(place, carry):
        for side in range(2):
            sent(place, side).wait()
        return carry

    lax.fori_loop(0, made.shape[0], step, 0)
    lax.fori_loop(0, made.shape[0], finish, 0)


def finish_sum(order, *terms):
    group, (rows, columns) = order.shape[0], terms[0].shape[1:]
    size = terms[0].size * 2
    return pl.pallas_call(
        finish_sum_kernel,
        out_shape=jax.ShapeDtypeStruct((group, 2, rows, columns // 2), bf16),
        in_specs=[whole_in(pltpu.SMEM)] + [whole_in(pltpu.VMEM)] * 4,
        out_specs=whole_in(pl.ANY),
        scratch_shapes=[pltpu.VMEM((group, rows, columns), bf16), pltpu.SemaphoreType.DMA((2,))],
        compiler_params=pltpu.CompilerParams(vmem_limit_bytes=16 << 20),
        cost_estimate=pl.CostEstimate(flops=size, bytes_accessed=6 * size, transcendentals=0),
        name="finish_sum",
    )(order, *terms)


def orient_kernel(
    core, root, root_halves, partner, partner_halves, left, right, left_in, right_in, sems
):
    shards, _, half_rows, size = left_in.shape
    mine = core[0]

    def left_copy(source):
        return pltpu.make_async_copy(source, left_in, sems.at[0])

    def right_copy(source):
        return pltpu.make_async_copy(source, right_in, sems.at[1])

    @pl.when(mine == 0)
    def _():
        left_copy(root).start()
        right_copy(partner_halves).start()

    @pl.when(mine == 1)
    def _():
        left_copy(partner).start()
        right_copy(root_halves).start()

    left_copy(root).wait()

    def place(shard, carry):
        rows = pl.ds(pl.multiple_of(shard * half_rows, half_rows), half_rows)
        left[0, rows, :] = left_in[shard, mine].astype(bf16)
        left[1, rows, :] = left_in[shard, 1 - mine].astype(bf16)
        return carry

    lax.fori_loop(0, shards, place, 0, unroll=4)
    right_copy(root_halves).wait()
    right[0] = right_in[mine].astype(bf16)
    right[1] = right_in[1 - mine].astype(bf16)


def oriented(core, root, partner, half_rows):
    size = root.shape[0]
    half = size // 2
    tall = (size // (2 * half_rows), 2, half_rows, size)
    root, partner = (
        (array.reshape(tall), array.reshape(2, half, size)) for array in (root, partner)
    )
    return pl.pallas_call(
        orient_kernel,
        out_shape=[jax.ShapeDtypeStruct((2, half, size), bf16)] * 2,
        in_specs=[whole_in(pltpu.SMEM)] + [whole_in(pl.ANY)] * 4,
        out_specs=[whole_in(pltpu.VMEM)] * 2,
        scratch_shapes=[
            pltpu.VMEM(tall, f32),
            pltpu.VMEM((2, half, size), f32),
            pltpu.SemaphoreType.DMA((2,)),
        ],
        compiler_params=pltpu.CompilerParams(vmem_limit_bytes=32 << 20),
        cost_estimate=pl.CostEstimate(flops=size**2, bytes_accessed=12 * size**2, transcendentals=0),
        name="orient",
    )(core, *root, *partner)


def begin_kernel(left, columns, kept, swapped):
    size, half = left.shape[2], left.shape[1]
    rows = columns[...].reshape(size, half)
    tile = half // 2
    for side, out in ((1, swapped), (0, kept)):
        for low in range(0, half, tile):
            out[low : low + tile, :] = jnp.dot(
                left[side, low : low + tile, :], rows, preferred_element_type=f32
            ).astype(bf16)


def begun(left, columns):
    half = left.shape[1]
    return pl.pallas_call(
        begin_kernel,
        out_shape=[jax.ShapeDtypeStruct((half, half), bf16)] * 2,
        in_specs=[whole_in(pltpu.VMEM)] * 2,
        out_specs=[whole_in(pltpu.VMEM)] * 2,
        compiler_params=pltpu.CompilerParams(vmem_limit_bytes=16 << 20),
        cost_estimate=pl.CostEstimate(flops=8 * half**3, bytes_accessed=16 * half**2, transcendentals=0),
        name="begin",
    )(left, columns)


def share_kernel(kept, right, part):
    size = part.shape[1]
    width = size // 4
    for low in range(0, size, width):
        columns = slice(low, low + width)
        part[:, columns] = jnp.dot(kept[...], right[0, :, columns], preferred_element_type=f32)


def shared(kept, right):
    half, size = right.shape[1:]
    return pl.pallas_call(
        share_kernel,
        out_shape=jax.ShapeDtypeStruct((half, size), f32),
        in_specs=[whole_in(pltpu.VMEM)] * 2,
        out_specs=whole_in(pltpu.VMEM),
        compiler_params=pltpu.CompilerParams(vmem_limit_bytes=16 << 20),
        cost_estimate=pl.CostEstimate(flops=4 * half**3, bytes_accessed=16 * half**2, transcendentals=0),
        name="share",
    )(kept, right)


def complete_kernel(part, other, right, update, made, sems):
    size = part.shape[1]
    width = size // 4
    copies = []
    for index, low in enumerate(range(0, size, width)):
        columns = slice(low, low + width)
        product = jnp.dot(other[...], right[1, :, columns], preferred_element_type=f32)
        made[:, columns] = (part[:, columns] + product).astype(bf16)
        copies.append(
            pltpu.make_async_copy(made.at[:, columns], update.at[:, columns], sems.at[index])
        )
        copies[-1].start()
    for copy in copies:
        copy.wait()


def completed(part, other, right):
    half, size = part.shape
    return pl.pallas_call(
        complete_kernel,
        out_shape=jax.ShapeDtypeStruct((half, size), bf16),
        in_specs=[whole_in(pltpu.VMEM)] * 3,
        out_specs=whole_in(pl.ANY),
        scratch_shapes=[pltpu.VMEM((half, size), bf16), pltpu.SemaphoreType.DMA((4,))],
        compiler_params=pltpu.CompilerParams(vmem_limit_bytes=16 << 20),
        cost_estimate=pl.CostEstimate(flops=4 * half**3, bytes_accessed=16 * half**2, transcendentals=0),
        name="complete",
    )(part, other, right)


def statistics_kernel(core, own, other, stat, out, gradient):
    size = gradient.shape[0]
    tile = stat.shape[0]
    step = pl.program_id(0)
    mine = core[0]

    @pl.when((step == 0) & (mine == 0))
    def _():
        gradient[:, : size // 2] = own[...].reshape(size, size // 2)
        gradient[:, size // 2 :] = other[...].reshape(size, size // 2)

    @pl.when((step == 0) & (mine == 1))
    def _():
        gradient[:, size // 2 :] = own[...].reshape(size, size // 2)
        gradient[:, : size // 2] = other[...].reshape(size, size // 2)

    rows = pl.ds(pl.multiple_of(step * tile, tile), tile)

    @pl.when(mine == 0)
    def _():
        outer = lax.dot_general(
            gradient[rows, :], gradient[...], (((1,), (1,)), ((), ())), preferred_element_type=f32
        )
        out[...] = keep_rate * stat[...] + (1.0 - keep_rate) / size * outer

    @pl.when(mine == 1)
    def _():
        outer = lax.dot_general(
            gradient[:, rows], gradient[...], (((0,), (0,)), ((), ())), preferred_element_type=f32
        )
        out[...] = keep_rate * stat[...] + (1.0 - keep_rate) / size * outer


def statistics(core, own, other, stat):
    size = stat.shape[0]
    tile = size // 4
    block = pl.BlockSpec((tile, size), lambda step: (step, 0))
    return pl.pallas_call(
        statistics_kernel,
        grid=(size // tile,),
        out_shape=jax.ShapeDtypeStruct(stat.shape, f32),
        in_specs=[whole_in(pltpu.SMEM)] + [whole_in(pltpu.VMEM)] * 2 + [block],
        out_specs=block,
        scratch_shapes=[pltpu.VMEM((size, size), bf16)],
        compiler_params=pltpu.CompilerParams(vmem_limit_bytes=16 << 20),
        cost_estimate=pl.CostEstimate(flops=2 * size**3, bytes_accessed=12 * size**2, transcendentals=0),
        name="statistics",
    )(core, own, other, stat)


def step_kernel(order, old, update, low, high):
    half = low.shape[0]

    def step(place, carry):
        block = order[place]
        fresh = old[block].astype(f32) - step_size * update[place].astype(f32)

        @pl.when(block < half)
        def _():
            low[block] = fresh.astype(bf16)

        @pl.when(block >= half)
        def _():
            high[block - half] = fresh.astype(bf16)

        return carry

    lax.fori_loop(0, old.shape[0], step, 0)


def stepped(order, old, update):
    shape = (old.shape[0] // 2,) + old.shape[1:]
    return pl.pallas_call(
        step_kernel,
        out_shape=[jax.ShapeDtypeStruct(shape, bf16)] * 2,
        in_specs=[whole_in(pltpu.SMEM)] + [whole_in(pltpu.VMEM)] * 2,
        out_specs=[whole_in(pltpu.VMEM)] * 2,
        compiler_params=pltpu.CompilerParams(vmem_limit_bytes=16 << 20),
        cost_estimate=pl.CostEstimate(flops=2 * old.size, bytes_accessed=6 * old.size, transcendentals=0),
        name="step",
    )(order, old, update)


def settle_kernel(replica, low_far, high_far, below, out, sems):
    half = low_far.shape[0]
    replicas = out.shape[0] // (2 * half)
    start = lax.rem(replica[0] + 2, replicas) * 2 * half
    copies = [
        pltpu.make_async_copy(piece, out.at[pl.ds(start + which * half, half)], sems.at[which])
        for which, piece in enumerate((low_far, high_far))
    ]
    for copy in copies:
        copy.start()
    for copy in copies:
        copy.wait()


def settled(replica, low_far, high_far, below):
    return pl.pallas_call(
        settle_kernel,
        out_shape=jax.ShapeDtypeStruct(below.shape, bf16),
        in_specs=[whole_in(pltpu.SMEM)] + [whole_in(pltpu.VMEM)] * 2 + [whole_in(pltpu.HBM)],
        out_specs=whole_in(pltpu.HBM),
        scratch_shapes=[pltpu.SemaphoreType.DMA((2,))],
        input_output_aliases={3: 0},
        compiler_params=pltpu.CompilerParams(vmem_limit_bytes=16 << 20),
        cost_estimate=pl.CostEstimate(flops=0, bytes_accessed=8 * low_far.size, transcendentals=0),
        name="settle",
    )(replica, low_far, high_far, below)


def on_device(grads, params, stats, roots, table):
    shards = lax.axis_size("shard")
    replicas = lax.axis_size("dp")
    blocks = grads.shape[1]
    group = blocks // replicas
    rows = grads.shape[2]
    size = grads.shape[3]
    half_rows = rows // 2
    half = group // 2
    replica = lax.axis_index("dp")
    core = (lax.axis_index("shard") % 2)[None]
    own_order = lax.dynamic_index_in_dim(table, replica, 0, keepdims=False)

    def piece(array, step, which):
        start = (replica + step) % replicas * group + which * half
        return lax.dynamic_slice_in_dim(array, start, half, 0)

    mine = grads[0]
    far = lax.optimization_barrier((piece(mine, 2, 0), piece(mine, 2, 1)))
    far_up = shifted(far[0], "dp", 1)
    far_down = shifted(far[1], "dp", -1)

    root = in_order((roots[0, 0],), far)[0]
    partner_root = other_core(root)
    mine = in_order((mine,), (partner_root,))[0]
    near = lax.optimization_barrier((piece(mine, 1, 1), piece(mine, 3, 0)))
    near_up = shifted(near[0], "dp", 1)
    near_down = shifted(near[1], "dp", -1)

    sums = lax.optimization_barrier(
        (added(piece(mine, 1, 0), far_up), added(piece(mine, 3, 1), far_down))
    )
    sum_up = shifted(sums[0], "dp", 1)
    sum_down = shifted(sums[1], "dp", -1)
    own, near_up, near_down = lax.optimization_barrier(
        (lax.dynamic_slice_in_dim(mine, replica * group, group, 0), near_up, near_down)
    )
    partial = lax.optimization_barrier((added(own[:half], near_down), added(own[half:], near_up)))
    root, partner_root = in_order((root, partner_root), partial)
    left, right = oriented(core, root, partner_root, half_rows)
    sum_up, sum_down, left, right = lax.optimization_barrier((sum_up, sum_down, left, right))
    whole = finish_sum(own_order, *partial, sum_up, sum_down)

    own_columns = exchanged(whole.reshape(shards, rows, size // 2))
    kept, swapped = begun(left, own_columns)
    swapped = other_core(swapped)
    part = shared(kept, right)
    update = completed(part, swapped, right)

    own_columns = in_order((own_columns,), (update,))[0]
    update = exchanged(update.reshape(shards, half_rows, size))
    other_columns = other_core(own_columns)
    new_stat = statistics(core, own_columns, other_columns, stats[0, 0])
    own_params = lax.dynamic_slice_in_dim(params, replica * group, group, 0)
    update, new_stat, own_params = lax.optimization_barrier((update, new_stat, own_params))
    low, high = stepped(own_order, own_params, update.reshape(group, rows, size))
    low_below = shifted(low, "dp", 1)
    high_above = shifted(high, "dp", -1)
    high_below = shifted(high, "dp", 1)
    low_above = shifted(low, "dp", -1)
    low_far = shifted(low_below, "dp", 1)
    high_far = shifted(high_above, "dp", -1)

    def placed(out, block, step, which):
        start = (replica + step) % replicas * group + which * half
        return lax.dynamic_update_slice_in_dim(out, block, start, 0)

    out = jnp.zeros(params.shape, bf16)
    out = placed(out, low_below, 3, 0)
    out = placed(out, high_above, 1, 1)
    out = placed(out, low, 0, 0)
    out = placed(out, high, 0, 1)
    out = placed(out, high_below, 3, 1)
    out = placed(out, low_above, 1, 0)
    out = settled(replica[None], low_far, high_far, out)
    return (out, new_stat[None, None])


def solution(mesh):
    placed = (
        P("dp", None, "shard", None),
        P(None, "shard", None),
        P("dp", "shard", None, None),
        P("dp", "shard", None, None),
        P(),
    )
    return jax.shard_map(
        on_device,
        mesh=mesh,
        in_specs=placed,
        out_specs=(P(None, "shard", None), P("dp", "shard", None, None)),
        check_vma=False,
    )
```

```python
import functools

import jax
import jax.numpy as jnp
from jax import lax
from jax.experimental import pallas as pl
from jax.experimental.pallas import tpu as pltpu
from jax.sharding import PartitionSpec as P

keep_rate = 0.75
step_size = 0.25
f32 = jnp.float32
bf16 = jnp.bfloat16


def shifted(block, axis, offset):
    count = lax.axis_size(axis)
    return lax.ppermute(block, axis, [(i, (i + offset) % count) for i in range(count)])


def other_core(block):
    count = lax.axis_size("shard")
    return lax.ppermute(block, "shard", [(i, i ^ 1) for i in range(count)])


def exchanged(blocks):
    return lax.all_to_all(blocks, "shard", split_axis=0, concat_axis=0, tiled=True)


def added(*terms):
    total = terms[0].astype(f32)
    for term in terms[1:]:
        total = total + term.astype(f32)
    return total.astype(bf16)


def in_order(values, after):
    held = lax.optimization_barrier(tuple(values) + tuple(after))
    return held[: len(values)]


def whole_in(space):
    return pl.BlockSpec(memory_space=space)


def finish_sum_kernel(order, low, high, sum_low, sum_high, out, made, sems):
    half = low.shape[0]
    columns = out.shape[3]

    def sent(place, side):
        source = made.at[place, :, pl.ds(side * columns, columns)]
        return pltpu.make_async_copy(source, out.at[place, side], sems.at[side])

    def step(place, carry):
        block = order[place]

        @pl.when(block < half)
        def _():
            made[place] = added(low[block], sum_low[block])

        @pl.when(block >= half)
        def _():
            made[place] = added(high[block - half], sum_high[block - half])

        for side in range(2):
            sent(place, side).start()
        return carry

    def finish(place, carry):
        for side in range(2):
            sent(place, side).wait()
        return carry

    lax.fori_loop(0, made.shape[0], step, 0, unroll=4)
    lax.fori_loop(0, made.shape[0], finish, 0, unroll=4)


def finish_sum(order, *terms):
    group, (rows, columns) = order.shape[0], terms[0].shape[1:]
    size = terms[0].size * 2
    return pl.pallas_call(
        finish_sum_kernel,
        out_shape=jax.ShapeDtypeStruct((group, 2, rows, columns // 2), bf16),
        in_specs=[whole_in(pltpu.SMEM)] + [whole_in(pltpu.VMEM)] * 4,
        out_specs=whole_in(pl.ANY),
        scratch_shapes=[pltpu.VMEM((group, rows, columns), bf16), pltpu.SemaphoreType.DMA((2,))],
        compiler_params=pltpu.CompilerParams(vmem_limit_bytes=16 << 20),
        cost_estimate=pl.CostEstimate(flops=size, bytes_accessed=6 * size, transcendentals=0),
        name="finish_sum",
    )(order, *terms)


def orient_kernel(
    core, root, root_halves, partner, partner_halves, left, right, left_in, right_in, sems
):
    shards, _, half_rows, size = left_in.shape
    mine = core[0]

    def left_copy(source):
        return pltpu.make_async_copy(source, left_in, sems.at[0])

    def right_copy(source):
        return pltpu.make_async_copy(source, right_in, sems.at[1])

    @pl.when(mine == 0)
    def _():
        left_copy(root).start()
        right_copy(partner_halves).start()

    @pl.when(mine == 1)
    def _():
        left_copy(partner).start()
        right_copy(root_halves).start()

    left_copy(root).wait()

    def place(shard, carry):
        rows = pl.ds(pl.multiple_of(shard * half_rows, half_rows), half_rows)
        left[0, rows, :] = left_in[shard, mine].astype(bf16)
        left[1, rows, :] = left_in[shard, 1 - mine].astype(bf16)
        return carry

    lax.fori_loop(0, shards, place, 0, unroll=4)
    right_copy(root_halves).wait()
    right[0] = right_in[mine].astype(bf16)
    right[1] = right_in[1 - mine].astype(bf16)


def oriented(core, root, partner, half_rows):
    size = root.shape[0]
    half = size // 2
    tall = (size // (2 * half_rows), 2, half_rows, size)
    root, partner = (
        (array.reshape(tall), array.reshape(2, half, size)) for array in (root, partner)
    )
    return pl.pallas_call(
        orient_kernel,
        out_shape=[jax.ShapeDtypeStruct((2, half, size), bf16)] * 2,
        in_specs=[whole_in(pltpu.SMEM)] + [whole_in(pl.ANY)] * 4,
        out_specs=[whole_in(pltpu.VMEM)] * 2,
        scratch_shapes=[
            pltpu.VMEM(tall, f32),
            pltpu.VMEM((2, half, size), f32),
            pltpu.SemaphoreType.DMA((2,)),
        ],
        compiler_params=pltpu.CompilerParams(vmem_limit_bytes=32 << 20),
        cost_estimate=pl.CostEstimate(flops=size**2, bytes_accessed=12 * size**2, transcendentals=0),
        name="orient",
    )(core, *root, *partner)


def begin_kernel(left, columns, swapped):
    half, size = left.shape[1:]
    rows = columns[...].reshape(size, half)
    tile = half // 2
    for low in range(0, half, tile):
        swapped[low : low + tile, :] = jnp.dot(
            left[1, low : low + tile, :], rows, preferred_element_type=f32
        ).astype(bf16)


def begun(left, columns):
    half = left.shape[1]
    return pl.pallas_call(
        begin_kernel,
        out_shape=jax.ShapeDtypeStruct((half, half), bf16),
        in_specs=[whole_in(pltpu.VMEM)] * 2,
        out_specs=whole_in(pltpu.VMEM),
        compiler_params=pltpu.CompilerParams(vmem_limit_bytes=16 << 20),
        cost_estimate=pl.CostEstimate(flops=4 * half**3, bytes_accessed=8 * half**2, transcendentals=0),
        name="begin",
    )(left, columns)


def share_kernel(left, columns, right, part, kept):
    half, size = left.shape[1:]
    rows = columns[...].reshape(size, half)
    tile = half // 2
    for low in range(0, half, tile):
        kept[low : low + tile, :] = jnp.dot(
            left[0, low : low + tile, :], rows, preferred_element_type=f32
        ).astype(bf16)
    for low in range(0, size, tile):
        part[:, low : low + tile] = jnp.dot(
            kept[...], right[0, :, low : low + tile], preferred_element_type=f32
        )


def shared(left, columns, right):
    half, size = right.shape[1:]
    return pl.pallas_call(
        share_kernel,
        out_shape=jax.ShapeDtypeStruct((half, size), f32),
        in_specs=[whole_in(pltpu.VMEM)] * 3,
        out_specs=whole_in(pltpu.VMEM),
        scratch_shapes=[pltpu.VMEM((half, half), bf16)],
        compiler_params=pltpu.CompilerParams(vmem_limit_bytes=16 << 20),
        cost_estimate=pl.CostEstimate(flops=8 * half**3, bytes_accessed=20 * half**2, transcendentals=0),
        name="share",
    )(left, columns, right)


def complete_kernel(part, other, right, update, made, sems):
    size = part.shape[1]
    width = size // 4
    copies = []
    for index, low in enumerate(range(0, size, width)):
        columns = slice(low, low + width)
        product = jnp.dot(other[...], right[1, :, columns], preferred_element_type=f32)
        made[:, columns] = (part[:, columns] + product).astype(bf16)
        copies.append(
            pltpu.make_async_copy(made.at[:, columns], update.at[:, columns], sems.at[index])
        )
        copies[-1].start()
    for copy in copies:
        copy.wait()


def completed(part, other, right):
    half, size = part.shape
    return pl.pallas_call(
        complete_kernel,
        out_shape=jax.ShapeDtypeStruct((half, size), bf16),
        in_specs=[whole_in(pltpu.VMEM)] * 3,
        out_specs=whole_in(pl.ANY),
        scratch_shapes=[pltpu.VMEM((half, size), bf16), pltpu.SemaphoreType.DMA((4,))],
        compiler_params=pltpu.CompilerParams(vmem_limit_bytes=16 << 20),
        cost_estimate=pl.CostEstimate(flops=4 * half**3, bytes_accessed=16 * half**2, transcendentals=0),
        name="complete",
    )(part, other, right)


def statistics_kernel(core, own, other, stat, out, gradient):
    size = gradient.shape[0]
    tile = stat.shape[0]
    step = pl.program_id(0)
    mine = core[0]

    @pl.when((step == 0) & (mine == 0))
    def _():
        gradient[:, : size // 2] = own[...].reshape(size, size // 2)
        gradient[:, size // 2 :] = other[...].reshape(size, size // 2)

    @pl.when((step == 0) & (mine == 1))
    def _():
        gradient[:, size // 2 :] = own[...].reshape(size, size // 2)
        gradient[:, : size // 2] = other[...].reshape(size, size // 2)

    rows = pl.ds(pl.multiple_of(step * tile, tile), tile)

    @pl.when(mine == 0)
    def _():
        outer = lax.dot_general(
            gradient[rows, :], gradient[...], (((1,), (1,)), ((), ())), preferred_element_type=f32
        )
        out[...] = keep_rate * stat[...] + (1.0 - keep_rate) / size * outer

    @pl.when(mine == 1)
    def _():
        outer = lax.dot_general(
            gradient[:, rows], gradient[...], (((0,), (0,)), ((), ())), preferred_element_type=f32
        )
        out[...] = keep_rate * stat[...] + (1.0 - keep_rate) / size * outer


def statistics(core, own, other, stat):
    size = stat.shape[0]
    tile = size // 4
    block = pl.BlockSpec((tile, size), lambda step: (step, 0))
    return pl.pallas_call(
        statistics_kernel,
        grid=(size // tile,),
        out_shape=jax.ShapeDtypeStruct(stat.shape, f32),
        in_specs=[whole_in(pltpu.SMEM)] + [whole_in(pltpu.VMEM)] * 2 + [block],
        out_specs=block,
        scratch_shapes=[pltpu.VMEM((size, size), bf16)],
        compiler_params=pltpu.CompilerParams(vmem_limit_bytes=16 << 20),
        cost_estimate=pl.CostEstimate(flops=2 * size**3, bytes_accessed=12 * size**2, transcendentals=0),
        name="statistics",
    )(core, own, other, stat)


def step_kernel(order, old, update, low, high):
    half = low.shape[0]

    def step(place, carry):
        block = order[place]
        fresh = old[block].astype(f32) - step_size * update[place].astype(f32)

        @pl.when(block < half)
        def _():
            low[block] = fresh.astype(bf16)

        @pl.when(block >= half)
        def _():
            high[block - half] = fresh.astype(bf16)

        return carry

    lax.fori_loop(0, old.shape[0], step, 0, unroll=4)


def stepped(order, old, update):
    shape = (old.shape[0] // 2,) + old.shape[1:]
    return pl.pallas_call(
        step_kernel,
        out_shape=[jax.ShapeDtypeStruct(shape, bf16)] * 2,
        in_specs=[whole_in(pltpu.SMEM)] + [whole_in(pltpu.VMEM)] * 2,
        out_specs=[whole_in(pltpu.VMEM)] * 2,
        compiler_params=pltpu.CompilerParams(vmem_limit_bytes=16 << 20),
        cost_estimate=pl.CostEstimate(flops=2 * old.size, bytes_accessed=6 * old.size, transcendentals=0),
        name="step",
    )(order, old, update)


def settle_kernel(replica, low_far, high_far, below, out, sems):
    half = low_far.shape[0]
    replicas = out.shape[0] // (2 * half)
    start = lax.rem(replica[0] + 2, replicas) * 2 * half
    copies = [
        pltpu.make_async_copy(piece, out.at[pl.ds(start + which * half, half)], sems.at[which])
        for which, piece in enumerate((low_far, high_far))
    ]
    for copy in copies:
        copy.start()
    for copy in copies:
        copy.wait()


def settled(replica, low_far, high_far, below):
    return pl.pallas_call(
        settle_kernel,
        out_shape=jax.ShapeDtypeStruct(below.shape, bf16),
        in_specs=[whole_in(pltpu.SMEM)] + [whole_in(pltpu.VMEM)] * 2 + [whole_in(pltpu.HBM)],
        out_specs=whole_in(pltpu.HBM),
        scratch_shapes=[pltpu.SemaphoreType.DMA((2,))],
        input_output_aliases={3: 0},
        compiler_params=pltpu.CompilerParams(vmem_limit_bytes=16 << 20),
        cost_estimate=pl.CostEstimate(flops=0, bytes_accessed=8 * low_far.size, transcendentals=0),
        name="settle",
    )(replica, low_far, high_far, below)


def on_device(grads, params, stats, roots, table):
    shards = lax.axis_size("shard")
    replicas = lax.axis_size("dp")
    blocks = grads.shape[1]
    group = blocks // replicas
    rows = grads.shape[2]
    size = grads.shape[3]
    half_rows = rows // 2
    half = group // 2
    replica = lax.axis_index("dp")
    core = (lax.axis_index("shard") % 2)[None]
    own_order = lax.dynamic_index_in_dim(table, replica, 0, keepdims=False)

    def piece(array, step, which):
        start = (replica + step) % replicas * group + which * half
        return lax.dynamic_slice_in_dim(array, start, half, 0)

    mine = grads[0]
    far = lax.optimization_barrier((piece(mine, 2, 0), piece(mine, 2, 1)))
    far_up = shifted(far[0], "dp", 1)
    far_down = shifted(far[1], "dp", -1)

    root = in_order((roots[0, 0],), far)[0]
    partner_root = other_core(root)
    mine = in_order((mine,), (partner_root,))[0]
    near = lax.optimization_barrier((piece(mine, 1, 1), piece(mine, 3, 0)))
    near_up = shifted(near[0], "dp", 1)
    near_down = shifted(near[1], "dp", -1)

    sums = lax.optimization_barrier(
        (added(piece(mine, 1, 0), far_up), added(piece(mine, 3, 1), far_down))
    )
    sum_up = shifted(sums[0], "dp", 1)
    sum_down = shifted(sums[1], "dp", -1)
    own, near_up, near_down = lax.optimization_barrier(
        (lax.dynamic_slice_in_dim(mine, replica * group, group, 0), near_up, near_down)
    )
    partial = lax.optimization_barrier((added(own[:half], near_down), added(own[half:], near_up)))
    root, partner_root = in_order((root, partner_root), partial)
    left, right = oriented(core, root, partner_root, half_rows)
    sum_up, sum_down, left, right = lax.optimization_barrier((sum_up, sum_down, left, right))
    whole = finish_sum(own_order, *partial, sum_up, sum_down)

    own_columns = exchanged(whole.reshape(shards, rows, size // 2))
    swapped = other_core(begun(left, own_columns))
    part = shared(left, own_columns, right)
    update = completed(part, swapped, right)

    own_columns = in_order((own_columns,), (update,))[0]
    update = exchanged(update.reshape(shards, half_rows, size))
    other_columns = other_core(own_columns)
    new_stat = statistics(core, own_columns, other_columns, stats[0, 0])
    own_params = lax.dynamic_slice_in_dim(params, replica * group, group, 0)
    update, new_stat, own_params = lax.optimization_barrier((update, new_stat, own_params))
    low, high = stepped(own_order, own_params, update.reshape(group, rows, size))
    low_below = shifted(low, "dp", 1)
    high_above = shifted(high, "dp", -1)
    high_below = shifted(high, "dp", 1)
    low_above = shifted(low, "dp", -1)
    low_far = shifted(low_below, "dp", 1)
    high_far = shifted(high_above, "dp", -1)

    def placed(out, block, step, which):
        start = (replica + step) % replicas * group + which * half
        return lax.dynamic_update_slice_in_dim(out, block, start, 0)

    out = jnp.zeros(params.shape, bf16)
    out = placed(out, low_below, 3, 0)
    out = placed(out, high_above, 1, 1)
    out = placed(out, low, 0, 0)
    out = placed(out, high, 0, 1)
    out = placed(out, high_below, 3, 1)
    out = placed(out, low_above, 1, 0)
    out = settled(replica[None], low_far, high_far, out)
    return (out, new_stat[None, None])


def solution(mesh):
    placed = (
        P("dp", None, "shard", None),
        P(None, "shard", None),
        P("dp", "shard", None, None),
        P("dp", "shard", None, None),
        P(),
    )
    return jax.shard_map(
        on_device,
        mesh=mesh,
        in_specs=placed,
        out_specs=(P(None, "shard", None), P("dp", "shard", None, None)),
        check_vma=False,
    )
```

```python
import functools

import jax
import jax.numpy as jnp
from jax import lax
from jax.experimental import pallas as pl
from jax.experimental.pallas import tpu as pltpu
from jax.sharding import PartitionSpec as P

keep_rate = 0.75
step_size = 0.25
f32 = jnp.float32
bf16 = jnp.bfloat16


def shifted(block, axis, offset):
    count = lax.axis_size(axis)
    return lax.ppermute(block, axis, [(i, (i + offset) % count) for i in range(count)])


def other_core(block):
    count = lax.axis_size("shard")
    return lax.ppermute(block, "shard", [(i, i ^ 1) for i in range(count)])


def exchanged(blocks):
    return lax.all_to_all(blocks, "shard", split_axis=0, concat_axis=0, tiled=True)


def added(*terms):
    total = terms[0].astype(f32)
    for term in terms[1:]:
        total = total + term.astype(f32)
    return total.astype(bf16)


def in_order(values, after):
    held = lax.optimization_barrier(tuple(values) + tuple(after))
    return held[: len(values)]


def whole_in(space):
    return pl.BlockSpec(memory_space=space)


def finish_sum_kernel(places, low, high, sum_low, sum_high, out, made, sems):
    half = low.shape[0]
    columns = out.shape[3]

    def sent(block, side):
        source = made.at[block, :, pl.ds(side * columns, columns)]
        return pltpu.make_async_copy(source, out.at[places[block], side], sems.at[side])

    for block in range(2 * half):
        partial, total = (low, sum_low) if block < half else (high, sum_high)
        made[block] = added(partial[block % half], total[block % half])
        for side in range(2):
            sent(block, side).start()
    for block in range(2 * half):
        for side in range(2):
            sent(block, side).wait()


def finish_sum(places, *terms):
    group, (rows, columns) = places.shape[0], terms[0].shape[1:]
    size = terms[0].size * 2
    return pl.pallas_call(
        finish_sum_kernel,
        out_shape=jax.ShapeDtypeStruct((group, 2, rows, columns // 2), bf16),
        in_specs=[whole_in(pltpu.SMEM)] + [whole_in(pltpu.VMEM)] * 4,
        out_specs=whole_in(pl.ANY),
        scratch_shapes=[pltpu.VMEM((group, rows, columns), bf16), pltpu.SemaphoreType.DMA((2,))],
        compiler_params=pltpu.CompilerParams(vmem_limit_bytes=16 << 20),
        cost_estimate=pl.CostEstimate(flops=size, bytes_accessed=6 * size, transcendentals=0),
        name="finish_sum",
    )(places, *terms)


def orient_kernel(
    core, root, root_halves, partner, partner_halves, left, right, left_in, right_in, sems
):
    shards, _, half_rows, size = left_in.shape
    mine = core[0]

    def left_copy(source):
        return pltpu.make_async_copy(source, left_in, sems.at[0])

    def right_copy(source):
        return pltpu.make_async_copy(source, right_in, sems.at[1])

    @pl.when(mine == 0)
    def _():
        left_copy(root).start()
        right_copy(partner_halves).start()

    @pl.when(mine == 1)
    def _():
        left_copy(partner).start()
        right_copy(root_halves).start()

    left_copy(root).wait()

    def place(shard, carry):
        rows = pl.ds(pl.multiple_of(shard * half_rows, half_rows), half_rows)
        left[0, rows, :] = left_in[shard, mine].astype(bf16)
        left[1, rows, :] = left_in[shard, 1 - mine].astype(bf16)
        return carry

    lax.fori_loop(0, shards, place, 0, unroll=4)
    right_copy(root_halves).wait()
    right[0] = right_in[mine].astype(bf16)
    right[1] = right_in[1 - mine].astype(bf16)


def oriented(core, root, partner, half_rows):
    size = root.shape[0]
    half = size // 2
    tall = (size // (2 * half_rows), 2, half_rows, size)
    root, partner = (
        (array.reshape(tall), array.reshape(2, half, size)) for array in (root, partner)
    )
    return pl.pallas_call(
        orient_kernel,
        out_shape=[jax.ShapeDtypeStruct((2, half, size), bf16)] * 2,
        in_specs=[whole_in(pltpu.SMEM)] + [whole_in(pl.ANY)] * 4,
        out_specs=[whole_in(pltpu.VMEM)] * 2,
        scratch_shapes=[
            pltpu.VMEM(tall, f32),
            pltpu.VMEM((2, half, size), f32),
            pltpu.SemaphoreType.DMA((2,)),
        ],
        compiler_params=pltpu.CompilerParams(vmem_limit_bytes=32 << 20),
        cost_estimate=pl.CostEstimate(flops=size**2, bytes_accessed=12 * size**2, transcendentals=0),
        name="orient",
    )(core, *root, *partner)


def begin_kernel(left, columns, swapped):
    half, size = left.shape[1:]
    rows = columns[...].reshape(size, half)
    tile = half // 2
    for low in range(0, half, tile):
        swapped[low : low + tile, :] = jnp.dot(
            left[1, low : low + tile, :], rows, preferred_element_type=f32
        ).astype(bf16)


def begun(left, columns):
    half = left.shape[1]
    return pl.pallas_call(
        begin_kernel,
        out_shape=jax.ShapeDtypeStruct((half, half), bf16),
        in_specs=[whole_in(pltpu.VMEM)] * 2,
        out_specs=whole_in(pltpu.VMEM),
        compiler_params=pltpu.CompilerParams(vmem_limit_bytes=16 << 20),
        cost_estimate=pl.CostEstimate(flops=4 * half**3, bytes_accessed=8 * half**2, transcendentals=0),
        name="begin",
    )(left, columns)


def share_kernel(left, columns, right, part, kept):
    half, size = left.shape[1:]
    rows = columns[...].reshape(size, half)
    tile = half // 2
    for low in range(0, half, tile):
        kept[low : low + tile, :] = jnp.dot(
            left[0, low : low + tile, :], rows, preferred_element_type=f32
        ).astype(bf16)
    for low in range(0, size, tile):
        part[:, low : low + tile] = jnp.dot(
            kept[...], right[0, :, low : low + tile], preferred_element_type=f32
        )


def shared(left, columns, right):
    half, size = right.shape[1:]
    return pl.pallas_call(
        share_kernel,
        out_shape=jax.ShapeDtypeStruct((half, size), f32),
        in_specs=[whole_in(pltpu.VMEM)] * 3,
        out_specs=whole_in(pltpu.VMEM),
        scratch_shapes=[pltpu.VMEM((half, half), bf16)],
        compiler_params=pltpu.CompilerParams(vmem_limit_bytes=16 << 20),
        cost_estimate=pl.CostEstimate(flops=8 * half**3, bytes_accessed=20 * half**2, transcendentals=0),
        name="share",
    )(left, columns, right)


def complete_kernel(part, other, right, update, made, sems):
    size = part.shape[1]
    width = size // 4
    copies = []
    for index, low in enumerate(range(0, size, width)):
        columns = slice(low, low + width)
        product = jnp.dot(other[...], right[1, :, columns], preferred_element_type=f32)
        made[:, columns] = (part[:, columns] + product).astype(bf16)
        copies.append(
            pltpu.make_async_copy(made.at[:, columns], update.at[:, columns], sems.at[index])
        )
        copies[-1].start()
    for copy in copies:
        copy.wait()


def completed(part, other, right):
    half, size = part.shape
    return pl.pallas_call(
        complete_kernel,
        out_shape=jax.ShapeDtypeStruct((half, size), bf16),
        in_specs=[whole_in(pltpu.VMEM)] * 3,
        out_specs=whole_in(pl.ANY),
        scratch_shapes=[pltpu.VMEM((half, size), bf16), pltpu.SemaphoreType.DMA((4,))],
        compiler_params=pltpu.CompilerParams(vmem_limit_bytes=16 << 20),
        cost_estimate=pl.CostEstimate(flops=4 * half**3, bytes_accessed=16 * half**2, transcendentals=0),
        name="complete",
    )(part, other, right)


def statistics_kernel(core, own, other, stat, out, gradient):
    size = gradient.shape[0]
    tile = stat.shape[0]
    step = pl.program_id(0)
    mine = core[0]

    @pl.when((step == 0) & (mine == 0))
    def _():
        gradient[:, : size // 2] = own[...].reshape(size, size // 2)
        gradient[:, size // 2 :] = other[...].reshape(size, size // 2)

    @pl.when((step == 0) & (mine == 1))
    def _():
        gradient[:, size // 2 :] = own[...].reshape(size, size // 2)
        gradient[:, : size // 2] = other[...].reshape(size, size // 2)

    rows = pl.ds(pl.multiple_of(step * tile, tile), tile)

    @pl.when(mine == 0)
    def _():
        outer = lax.dot_general(
            gradient[rows, :], gradient[...], (((1,), (1,)), ((), ())), preferred_element_type=f32
        )
        out[...] = keep_rate * stat[...] + (1.0 - keep_rate) / size * outer

    @pl.when(mine == 1)
    def _():
        outer = lax.dot_general(
            gradient[:, rows], gradient[...], (((0,), (0,)), ((), ())), preferred_element_type=f32
        )
        out[...] = keep_rate * stat[...] + (1.0 - keep_rate) / size * outer


def statistics(core, own, other, stat):
    size = stat.shape[0]
    tile = size // 4
    block = pl.BlockSpec((tile, size), lambda step: (step, 0))
    return pl.pallas_call(
        statistics_kernel,
        grid=(size // tile,),
        out_shape=jax.ShapeDtypeStruct(stat.shape, f32),
        in_specs=[whole_in(pltpu.SMEM)] + [whole_in(pltpu.VMEM)] * 2 + [block],
        out_specs=block,
        scratch_shapes=[pltpu.VMEM((size, size), bf16)],
        compiler_params=pltpu.CompilerParams(vmem_limit_bytes=16 << 20),
        cost_estimate=pl.CostEstimate(flops=2 * size**3, bytes_accessed=12 * size**2, transcendentals=0),
        name="statistics",
    )(core, own, other, stat)


def step_kernel(places, old, update, low, high):
    half = low.shape[0]
    for block in range(2 * half):
        fresh = old[block].astype(f32) - step_size * update[places[block]].astype(f32)
        out = low if block < half else high
        out[block % half] = fresh.astype(bf16)


def stepped(places, old, update):
    shape = (old.shape[0] // 2,) + old.shape[1:]
    return pl.pallas_call(
        step_kernel,
        out_shape=[jax.ShapeDtypeStruct(shape, bf16)] * 2,
        in_specs=[whole_in(pltpu.SMEM)] + [whole_in(pltpu.VMEM)] * 2,
        out_specs=[whole_in(pltpu.VMEM)] * 2,
        compiler_params=pltpu.CompilerParams(vmem_limit_bytes=16 << 20),
        cost_estimate=pl.CostEstimate(flops=2 * old.size, bytes_accessed=6 * old.size, transcendentals=0),
        name="step",
    )(places, old, update)


def settle_kernel(replica, low_far, high_far, below, out, sems):
    half = low_far.shape[0]
    replicas = out.shape[0] // (2 * half)
    start = lax.rem(replica[0] + 2, replicas) * 2 * half
    copies = [
        pltpu.make_async_copy(piece, out.at[pl.ds(start + which * half, half)], sems.at[which])
        for which, piece in enumerate((low_far, high_far))
    ]
    for copy in copies:
        copy.start()
    for copy in copies:
        copy.wait()


def settled(replica, low_far, high_far, below):
    return pl.pallas_call(
        settle_kernel,
        out_shape=jax.ShapeDtypeStruct(below.shape, bf16),
        in_specs=[whole_in(pltpu.SMEM)] + [whole_in(pltpu.VMEM)] * 2 + [whole_in(pltpu.HBM)],
        out_specs=whole_in(pltpu.HBM),
        scratch_shapes=[pltpu.SemaphoreType.DMA((2,))],
        input_output_aliases={3: 0},
        compiler_params=pltpu.CompilerParams(vmem_limit_bytes=16 << 20),
        cost_estimate=pl.CostEstimate(flops=0, bytes_accessed=8 * low_far.size, transcendentals=0),
        name="settle",
    )(replica, low_far, high_far, below)


def on_device(grads, params, stats, roots, table):
    shards = lax.axis_size("shard")
    replicas = lax.axis_size("dp")
    blocks = grads.shape[1]
    group = blocks // replicas
    rows = grads.shape[2]
    size = grads.shape[3]
    half_rows = rows // 2
    half = group // 2
    replica = lax.axis_index("dp")
    core = (lax.axis_index("shard") % 2)[None]
    own_order = lax.dynamic_index_in_dim(table, replica, 0, keepdims=False)
    numbers = jnp.arange(group, dtype=table.dtype)
    own_places = jnp.max(
        jnp.where(own_order[None, :] == numbers[:, None], numbers[None, :], 0), axis=1
    )

    def piece(array, step, which):
        start = (replica + step) % replicas * group + which * half
        return lax.dynamic_slice_in_dim(array, start, half, 0)

    mine = grads[0]
    far = lax.optimization_barrier((piece(mine, 2, 0), piece(mine, 2, 1)))
    far_up = shifted(far[0], "dp", 1)
    far_down = shifted(far[1], "dp", -1)

    root = in_order((roots[0, 0],), far)[0]
    partner_root = other_core(root)
    mine = in_order((mine,), (partner_root,))[0]
    near = lax.optimization_barrier((piece(mine, 1, 1), piece(mine, 3, 0)))
    near_up = shifted(near[0], "dp", 1)
    near_down = shifted(near[1], "dp", -1)

    sums = lax.optimization_barrier(
        (added(piece(mine, 1, 0), far_up), added(piece(mine, 3, 1), far_down))
    )
    sum_up = shifted(sums[0], "dp", 1)
    sum_down = shifted(sums[1], "dp", -1)
    own, near_up, near_down = lax.optimization_barrier(
        (lax.dynamic_slice_in_dim(mine, replica * group, group, 0), near_up, near_down)
    )
    partial = lax.optimization_barrier((added(own[:half], near_down), added(own[half:], near_up)))
    root, partner_root = in_order((root, partner_root), partial)
    left, right = oriented(core, root, partner_root, half_rows)
    sum_up, sum_down, left, right = lax.optimization_barrier((sum_up, sum_down, left, right))
    whole = finish_sum(own_places, *partial, sum_up, sum_down)

    own_columns = exchanged(whole.reshape(shards, rows, size // 2))
    swapped = other_core(begun(left, own_columns))
    part = shared(left, own_columns, right)
    update = completed(part, swapped, right)

    own_columns = in_order((own_columns,), (update,))[0]
    update = exchanged(update.reshape(shards, half_rows, size))
    other_columns = other_core(own_columns)
    new_stat = statistics(core, own_columns, other_columns, stats[0, 0])
    own_params = lax.dynamic_slice_in_dim(params, replica * group, group, 0)
    update, new_stat, own_params = lax.optimization_barrier((update, new_stat, own_params))
    low, high = stepped(own_places, own_params, update.reshape(group, rows, size))
    low_below = shifted(low, "dp", 1)
    high_above = shifted(high, "dp", -1)
    high_below = shifted(high, "dp", 1)
    low_above = shifted(low, "dp", -1)
    low_far = shifted(low_below, "dp", 1)
    high_far = shifted(high_above, "dp", -1)

    def placed(out, block, step, which):
        start = (replica + step) % replicas * group + which * half
        return lax.dynamic_update_slice_in_dim(out, block, start, 0)

    out = jnp.zeros(params.shape, bf16)
    out = placed(out, low_below, 3, 0)
    out = placed(out, high_above, 1, 1)
    out = placed(out, low, 0, 0)
    out = placed(out, high, 0, 1)
    out = placed(out, high_below, 3, 1)
    out = placed(out, low_above, 1, 0)
    out = settled(replica[None], low_far, high_far, out)
    return (out, new_stat[None, None])


def solution(mesh):
    placed = (
        P("dp", None, "shard", None),
        P(None, "shard", None),
        P("dp", "shard", None, None),
        P("dp", "shard", None, None),
        P(),
    )
    return jax.shard_map(
        on_device,
        mesh=mesh,
        in_specs=placed,
        out_specs=(P(None, "shard", None), P("dp", "shard", None, None)),
        check_vma=False,
    )
```

```python
import functools

import jax
import jax.numpy as jnp
from jax import lax
from jax.experimental import pallas as pl
from jax.experimental.pallas import tpu as pltpu
from jax.sharding import PartitionSpec as P

keep_rate = 0.75
step_size = 0.25
f32 = jnp.float32
bf16 = jnp.bfloat16


def shifted(block, axis, offset):
    count = lax.axis_size(axis)
    return lax.ppermute(block, axis, [(i, (i + offset) % count) for i in range(count)])


def other_core(block):
    count = lax.axis_size("shard")
    return lax.ppermute(block, "shard", [(i, i ^ 1) for i in range(count)])


def exchanged(blocks):
    return lax.all_to_all(blocks, "shard", split_axis=0, concat_axis=0, tiled=True)


def added(*terms):
    total = terms[0].astype(f32)
    for term in terms[1:]:
        total = total + term.astype(f32)
    return total.astype(bf16)


def in_order(values, after):
    held = lax.optimization_barrier(tuple(values) + tuple(after))
    return held[: len(values)]


def whole_in(space):
    return pl.BlockSpec(memory_space=space)


def finish_sum_kernel(places, low, high, sum_low, sum_high, out, made, sems):
    half = low.shape[0]
    columns = out.shape[3]

    def sent(block, side):
        source = made.at[block, :, pl.ds(side * columns, columns)]
        return pltpu.make_async_copy(source, out.at[places[block], side], sems.at[side])

    for block in range(2 * half):
        partial, total = (low, sum_low) if block < half else (high, sum_high)
        made[block] = added(partial[block % half], total[block % half])
        for side in range(2):
            sent(block, side).start()
    for block in range(2 * half):
        for side in range(2):
            sent(block, side).wait()


def finish_sum(places, *terms):
    group, (rows, columns) = places.shape[0], terms[0].shape[1:]
    size = terms[0].size * 2
    return pl.pallas_call(
        finish_sum_kernel,
        out_shape=jax.ShapeDtypeStruct((group, 2, rows, columns // 2), bf16),
        in_specs=[whole_in(pltpu.SMEM)] + [whole_in(pltpu.VMEM)] * 4,
        out_specs=whole_in(pl.ANY),
        scratch_shapes=[pltpu.VMEM((group, rows, columns), bf16), pltpu.SemaphoreType.DMA((2,))],
        compiler_params=pltpu.CompilerParams(vmem_limit_bytes=16 << 20),
        cost_estimate=pl.CostEstimate(flops=size, bytes_accessed=6 * size, transcendentals=0),
        name="finish_sum",
    )(places, *terms)


def orient_kernel(
    core, root, root_halves, partner, partner_halves, left, right, left_in, right_in, sems
):
    shards, _, half_rows, size = left_in.shape
    mine = core[0]

    def left_copy(source):
        return pltpu.make_async_copy(source, left_in, sems.at[0])

    def right_copy(source):
        return pltpu.make_async_copy(source, right_in, sems.at[1])

    @pl.when(mine == 0)
    def _():
        left_copy(root).start()
        right_copy(partner_halves).start()

    @pl.when(mine == 1)
    def _():
        left_copy(partner).start()
        right_copy(root_halves).start()

    left_copy(root).wait()

    def place(shard, carry):
        rows = pl.ds(pl.multiple_of(shard * half_rows, half_rows), half_rows)
        left[0, rows, :] = left_in[shard, mine].astype(bf16)
        left[1, rows, :] = left_in[shard, 1 - mine].astype(bf16)
        return carry

    lax.fori_loop(0, shards, place, 0, unroll=4)
    right_copy(root_halves).wait()
    right[0] = right_in[mine].astype(bf16)
    right[1] = right_in[1 - mine].astype(bf16)


def oriented(core, root, partner, half_rows):
    size = root.shape[0]
    half = size // 2
    tall = (size // (2 * half_rows), 2, half_rows, size)
    root, partner = (
        (array.reshape(tall), array.reshape(2, half, size)) for array in (root, partner)
    )
    return pl.pallas_call(
        orient_kernel,
        out_shape=[jax.ShapeDtypeStruct((2, half, size), bf16)] * 2,
        in_specs=[whole_in(pltpu.SMEM)] + [whole_in(pl.ANY)] * 4,
        out_specs=[whole_in(pltpu.VMEM)] * 2,
        scratch_shapes=[
            pltpu.VMEM(tall, f32),
            pltpu.VMEM((2, half, size), f32),
            pltpu.SemaphoreType.DMA((2,)),
        ],
        compiler_params=pltpu.CompilerParams(vmem_limit_bytes=32 << 20),
        cost_estimate=pl.CostEstimate(flops=size**2, bytes_accessed=12 * size**2, transcendentals=0),
        name="orient",
    )(core, *root, *partner)


def begin_kernel(left, columns, swapped):
    half, size = left.shape[1:]
    rows = columns[...].reshape(size, half)
    tile = half // 2
    for low in range(0, half, tile):
        swapped[low : low + tile, :] = jnp.dot(
            left[1, low : low + tile, :], rows, preferred_element_type=f32
        ).astype(bf16)


def begun(left, columns):
    half = left.shape[1]
    return pl.pallas_call(
        begin_kernel,
        out_shape=jax.ShapeDtypeStruct((half, half), bf16),
        in_specs=[whole_in(pltpu.VMEM)] * 2,
        out_specs=whole_in(pltpu.VMEM),
        compiler_params=pltpu.CompilerParams(vmem_limit_bytes=16 << 20),
        cost_estimate=pl.CostEstimate(flops=4 * half**3, bytes_accessed=8 * half**2, transcendentals=0),
        name="begin",
    )(left, columns)


def share_kernel(left, columns, right, part, kept):
    half, size = left.shape[1:]
    rows = columns[...].reshape(size, half)
    tile = half // 2
    for low in range(0, half, tile):
        kept[low : low + tile, :] = jnp.dot(
            left[0, low : low + tile, :], rows, preferred_element_type=f32
        ).astype(bf16)
    for low in range(0, size, tile):
        part[:, low : low + tile] = jnp.dot(
            kept[...], right[0, :, low : low + tile], preferred_element_type=f32
        )


def shared(left, columns, right):
    half, size = right.shape[1:]
    return pl.pallas_call(
        share_kernel,
        out_shape=jax.ShapeDtypeStruct((half, size), f32),
        in_specs=[whole_in(pltpu.VMEM)] * 3,
        out_specs=whole_in(pltpu.VMEM),
        scratch_shapes=[pltpu.VMEM((half, half), bf16)],
        compiler_params=pltpu.CompilerParams(vmem_limit_bytes=16 << 20),
        cost_estimate=pl.CostEstimate(flops=8 * half**3, bytes_accessed=20 * half**2, transcendentals=0),
        name="share",
    )(left, columns, right)


def complete_kernel(part, other, right, update, made, sems):
    size = part.shape[1]
    width = size // 4
    copies = []
    for index, low in enumerate(range(0, size, width)):
        columns = slice(low, low + width)
        product = jnp.dot(other[...], right[1, :, columns], preferred_element_type=f32)
        made[:, columns] = (part[:, columns] + product).astype(bf16)
        copies.append(
            pltpu.make_async_copy(made.at[:, columns], update.at[:, columns], sems.at[index])
        )
        copies[-1].start()
    for copy in copies:
        copy.wait()


def completed(part, other, right):
    half, size = part.shape
    return pl.pallas_call(
        complete_kernel,
        out_shape=jax.ShapeDtypeStruct((half, size), bf16),
        in_specs=[whole_in(pltpu.VMEM)] * 3,
        out_specs=whole_in(pl.ANY),
        scratch_shapes=[pltpu.VMEM((half, size), bf16), pltpu.SemaphoreType.DMA((4,))],
        compiler_params=pltpu.CompilerParams(vmem_limit_bytes=16 << 20),
        cost_estimate=pl.CostEstimate(flops=4 * half**3, bytes_accessed=16 * half**2, transcendentals=0),
        name="complete",
    )(part, other, right)


def statistics_kernel(core, own, other, stat, out, gradient):
    size = gradient.shape[0]
    tile = stat.shape[0]
    step = pl.program_id(0)
    mine = core[0]

    @pl.when((step == 0) & (mine == 0))
    def _():
        gradient[:, : size // 2] = own[...].reshape(size, size // 2)
        gradient[:, size // 2 :] = other[...].reshape(size, size // 2)

    @pl.when((step == 0) & (mine == 1))
    def _():
        gradient[:, size // 2 :] = own[...].reshape(size, size // 2)
        gradient[:, : size // 2] = other[...].reshape(size, size // 2)

    rows = pl.ds(pl.multiple_of(step * tile, tile), tile)

    @pl.when(mine == 0)
    def _():
        outer = lax.dot_general(
            gradient[rows, :], gradient[...], (((1,), (1,)), ((), ())), preferred_element_type=f32
        )
        out[...] = keep_rate * stat[...] + (1.0 - keep_rate) / size * outer

    @pl.when(mine == 1)
    def _():
        outer = lax.dot_general(
            gradient[:, rows], gradient[...], (((0,), (0,)), ((), ())), preferred_element_type=f32
        )
        out[...] = keep_rate * stat[...] + (1.0 - keep_rate) / size * outer


def statistics(core, own, other, stat):
    size = stat.shape[0]
    tile = size // 4
    block = pl.BlockSpec((tile, size), lambda step: (step, 0))
    return pl.pallas_call(
        statistics_kernel,
        grid=(size // tile,),
        out_shape=jax.ShapeDtypeStruct(stat.shape, f32),
        in_specs=[whole_in(pltpu.SMEM)] + [whole_in(pltpu.VMEM)] * 2 + [block],
        out_specs=block,
        scratch_shapes=[pltpu.VMEM((size, size), bf16)],
        compiler_params=pltpu.CompilerParams(vmem_limit_bytes=16 << 20),
        cost_estimate=pl.CostEstimate(flops=2 * size**3, bytes_accessed=12 * size**2, transcendentals=0),
        name="statistics",
    )(core, own, other, stat)


def step_kernel(places, old, update, low, high):
    half = low.shape[0]
    for block in range(2 * half):
        fresh = old[block].astype(f32) - step_size * update[places[block]].astype(f32)
        out = low if block < half else high
        out[block % half] = fresh.astype(bf16)


def stepped(places, old, update):
    shape = (old.shape[0] // 2,) + old.shape[1:]
    return pl.pallas_call(
        step_kernel,
        out_shape=[jax.ShapeDtypeStruct(shape, bf16)] * 2,
        in_specs=[whole_in(pltpu.SMEM)] + [whole_in(pltpu.VMEM)] * 2,
        out_specs=[whole_in(pltpu.VMEM)] * 2,
        compiler_params=pltpu.CompilerParams(vmem_limit_bytes=16 << 20),
        cost_estimate=pl.CostEstimate(flops=2 * old.size, bytes_accessed=6 * old.size, transcendentals=0),
        name="step",
    )(places, old, update)


def settle_kernel(replica, low_far, high_far, below, out, sems):
    half = low_far.shape[0]
    replicas = out.shape[0] // (2 * half)
    start = lax.rem(replica[0] + 2, replicas) * 2 * half
    copies = [
        pltpu.make_async_copy(piece, out.at[pl.ds(start + which * half, half)], sems.at[which])
        for which, piece in enumerate((low_far, high_far))
    ]
    for copy in copies:
        copy.start()
    for copy in copies:
        copy.wait()


def settled(replica, low_far, high_far, below):
    return pl.pallas_call(
        settle_kernel,
        out_shape=jax.ShapeDtypeStruct(below.shape, bf16),
        in_specs=[whole_in(pltpu.SMEM)] + [whole_in(pltpu.VMEM)] * 2 + [whole_in(pltpu.HBM)],
        out_specs=whole_in(pltpu.HBM),
        scratch_shapes=[pltpu.SemaphoreType.DMA((2,))],
        input_output_aliases={3: 0},
        compiler_params=pltpu.CompilerParams(vmem_limit_bytes=16 << 20),
        cost_estimate=pl.CostEstimate(flops=0, bytes_accessed=8 * low_far.size, transcendentals=0),
        name="settle",
    )(replica, low_far, high_far, below)


def on_device(grads, params, stats, roots, table):
    shards = lax.axis_size("shard")
    replicas = lax.axis_size("dp")
    blocks = grads.shape[1]
    group = blocks // replicas
    rows = grads.shape[2]
    size = grads.shape[3]
    half_rows = rows // 2
    half = group // 2
    replica = lax.axis_index("dp")
    core = (lax.axis_index("shard") % 2)[None]
    own_order = lax.dynamic_index_in_dim(table, replica, 0, keepdims=False)
    numbers = jnp.arange(group, dtype=table.dtype)
    own_places = jnp.max(
        jnp.where(own_order[None, :] == numbers[:, None], numbers[None, :], 0), axis=1
    )

    def piece(array, step, which):
        start = (replica + step) % replicas * group + which * half
        return lax.dynamic_slice_in_dim(array, start, half, 0)

    mine = grads[0]
    far = lax.optimization_barrier((piece(mine, 2, 0), piece(mine, 2, 1)))
    far_up = shifted(far[0], "dp", 1)
    far_down = shifted(far[1], "dp", -1)

    root = in_order((roots[0, 0],), far)[0]
    partner_root = other_core(root)
    mine = in_order((mine,), (partner_root,))[0]
    near = lax.optimization_barrier((piece(mine, 1, 1), piece(mine, 3, 0)))
    near_up = shifted(near[0], "dp", 1)
    near_down = shifted(near[1], "dp", -1)

    sum_up = shifted(added(piece(mine, 1, 0), far_up), "dp", 1)
    sum_down = shifted(added(piece(mine, 3, 1), far_down), "dp", -1)
    own, near_up, near_down = lax.optimization_barrier(
        (lax.dynamic_slice_in_dim(mine, replica * group, group, 0), near_up, near_down)
    )
    partial = lax.optimization_barrier((added(own[:half], near_down), added(own[half:], near_up)))
    root, partner_root = in_order((root, partner_root), partial)
    left, right = oriented(core, root, partner_root, half_rows)
    sum_up, sum_down, left, right = lax.optimization_barrier((sum_up, sum_down, left, right))
    whole = finish_sum(own_places, *partial, sum_up, sum_down)

    own_columns = exchanged(whole.reshape(shards, rows, size // 2))
    swapped = other_core(begun(left, own_columns))
    part = shared(left, own_columns, right)
    update = completed(part, swapped, right)

    own_columns = in_order((own_columns,), (update,))[0]
    update = exchanged(update.reshape(shards, half_rows, size))
    other_columns = other_core(own_columns)
    new_stat = statistics(core, own_columns, other_columns, stats[0, 0])
    own_params = lax.dynamic_slice_in_dim(params, replica * group, group, 0)
    update, new_stat, own_params = lax.optimization_barrier((update, new_stat, own_params))
    low, high = stepped(own_places, own_params, update.reshape(group, rows, size))
    low_below = shifted(low, "dp", 1)
    high_above = shifted(high, "dp", -1)
    high_below = shifted(high, "dp", 1)
    low_above = shifted(low, "dp", -1)
    low_far = shifted(low_below, "dp", 1)
    high_far = shifted(high_above, "dp", -1)

    def placed(out, block, step, which):
        start = (replica + step) % replicas * group + which * half
        return lax.dynamic_update_slice_in_dim(out, block, start, 0)

    out = jnp.zeros(params.shape, bf16)
    out = placed(out, low_below, 3, 0)
    out = placed(out, high_above, 1, 1)
    out = placed(out, low, 0, 0)
    out = placed(out, high, 0, 1)
    out = placed(out, high_below, 3, 1)
    out = placed(out, low_above, 1, 0)
    out = settled(replica[None], low_far, high_far, out)
    return (out, new_stat[None, None])


def solution(mesh):
    placed = (
        P("dp", None, "shard", None),
        P(None, "shard", None),
        P("dp", "shard", None, None),
        P("dp", "shard", None, None),
        P(),
    )
    return jax.shard_map(
        on_device,
        mesh=mesh,
        in_specs=placed,
        out_specs=(P(None, "shard", None), P("dp", "shard", None, None)),
        check_vma=False,
    )
```

```python
import functools

import jax
import jax.numpy as jnp
from jax import lax
from jax.experimental import pallas as pl
from jax.experimental.pallas import tpu as pltpu
from jax.sharding import PartitionSpec as P

keep_rate = 0.75
step_size = 0.25
f32 = jnp.float32
bf16 = jnp.bfloat16


def shifted(block, axis, offset):
    count = lax.axis_size(axis)
    return lax.ppermute(block, axis, [(i, (i + offset) % count) for i in range(count)])


def other_core(block):
    count = lax.axis_size("shard")
    return lax.ppermute(block, "shard", [(i, i ^ 1) for i in range(count)])


def exchanged(blocks):
    return lax.all_to_all(blocks, "shard", split_axis=0, concat_axis=0, tiled=True)


def added(*terms):
    total = terms[0].astype(f32)
    for term in terms[1:]:
        total = total + term.astype(f32)
    return total.astype(bf16)


def in_order(values, after):
    held = lax.optimization_barrier(tuple(values) + tuple(after))
    return held[: len(values)]


def whole_in(space):
    return pl.BlockSpec(memory_space=space)


def finish_sum_kernel(places, low, high, sum_low, sum_high, out, made, sems):
    half = low.shape[0]
    columns = out.shape[3]

    def sent(block, side):
        source = made.at[block, :, pl.ds(side * columns, columns)]
        return pltpu.make_async_copy(source, out.at[places[block], side], sems.at[side])

    for block in range(2 * half):
        partial, total = (low, sum_low) if block < half else (high, sum_high)
        made[block] = added(partial[block % half], total[block % half])
        for side in range(2):
            sent(block, side).start()
    for block in range(2 * half):
        for side in range(2):
            sent(block, side).wait()


def finish_sum(places, *terms):
    group, (rows, columns) = places.shape[0], terms[0].shape[1:]
    size = terms[0].size * 2
    return pl.pallas_call(
        finish_sum_kernel,
        out_shape=jax.ShapeDtypeStruct((group, 2, rows, columns // 2), bf16),
        in_specs=[whole_in(pltpu.SMEM)] + [whole_in(pltpu.VMEM)] * 4,
        out_specs=whole_in(pl.ANY),
        scratch_shapes=[pltpu.VMEM((group, rows, columns), bf16), pltpu.SemaphoreType.DMA((2,))],
        compiler_params=pltpu.CompilerParams(vmem_limit_bytes=16 << 20),
        cost_estimate=pl.CostEstimate(flops=size, bytes_accessed=6 * size, transcendentals=0),
        name="finish_sum",
    )(places, *terms)


def orient_kernel(
    core, root, root_halves, partner, partner_halves, left, right, left_in, right_in, sems
):
    shards, _, half_rows, size = left_in.shape
    mine = core[0]

    def left_copy(source):
        return pltpu.make_async_copy(source, left_in, sems.at[0])

    def right_copy(source):
        return pltpu.make_async_copy(source, right_in, sems.at[1])

    @pl.when(mine == 0)
    def _():
        left_copy(root).start()
        right_copy(partner_halves).start()

    @pl.when(mine == 1)
    def _():
        left_copy(partner).start()
        right_copy(root_halves).start()

    left_copy(root).wait()

    def place(shard, carry):
        rows = pl.ds(pl.multiple_of(shard * half_rows, half_rows), half_rows)
        left[0, rows, :] = left_in[shard, mine].astype(bf16)
        left[1, rows, :] = left_in[shard, 1 - mine].astype(bf16)
        return carry

    lax.fori_loop(0, shards, place, 0, unroll=4)
    right_copy(root_halves).wait()
    right[0] = right_in[mine].astype(bf16)
    right[1] = right_in[1 - mine].astype(bf16)


def oriented(core, root, partner, half_rows):
    size = root.shape[0]
    half = size // 2
    tall = (size // (2 * half_rows), 2, half_rows, size)
    root, partner = (
        (array.reshape(tall), array.reshape(2, half, size)) for array in (root, partner)
    )
    return pl.pallas_call(
        orient_kernel,
        out_shape=[jax.ShapeDtypeStruct((2, half, size), bf16)] * 2,
        in_specs=[whole_in(pltpu.SMEM)] + [whole_in(pl.ANY)] * 4,
        out_specs=[whole_in(pltpu.VMEM)] * 2,
        scratch_shapes=[
            pltpu.VMEM(tall, f32),
            pltpu.VMEM((2, half, size), f32),
            pltpu.SemaphoreType.DMA((2,)),
        ],
        compiler_params=pltpu.CompilerParams(vmem_limit_bytes=32 << 20),
        cost_estimate=pl.CostEstimate(flops=size**2, bytes_accessed=12 * size**2, transcendentals=0),
        name="orient",
    )(core, *root, *partner)


def begin_kernel(left, columns, swapped):
    half, size = left.shape[1:]
    rows = columns[...].reshape(size, half)
    tile = half // 2
    for low in range(0, half, tile):
        swapped[low : low + tile, :] = jnp.dot(
            left[1, low : low + tile, :], rows, preferred_element_type=f32
        ).astype(bf16)


def begun(left, columns):
    half = left.shape[1]
    return pl.pallas_call(
        begin_kernel,
        out_shape=jax.ShapeDtypeStruct((half, half), bf16),
        in_specs=[whole_in(pltpu.VMEM)] * 2,
        out_specs=whole_in(pltpu.VMEM),
        compiler_params=pltpu.CompilerParams(vmem_limit_bytes=16 << 20),
        cost_estimate=pl.CostEstimate(flops=4 * half**3, bytes_accessed=8 * half**2, transcendentals=0),
        name="begin",
    )(left, columns)


def share_kernel(left, columns, right, part, kept):
    half, size = left.shape[1:]
    rows = columns[...].reshape(size, half)
    tile = half // 2
    for low in range(0, half, tile):
        kept[low : low + tile, :] = jnp.dot(
            left[0, low : low + tile, :], rows, preferred_element_type=f32
        ).astype(bf16)
    for low in range(0, size, tile):
        part[:, low : low + tile] = jnp.dot(
            kept[...], right[0, :, low : low + tile], preferred_element_type=f32
        ).astype(bf16)


def shared(left, columns, right):
    half, size = right.shape[1:]
    return pl.pallas_call(
        share_kernel,
        out_shape=jax.ShapeDtypeStruct((half, size), bf16),
        in_specs=[whole_in(pltpu.VMEM)] * 3,
        out_specs=whole_in(pltpu.VMEM),
        scratch_shapes=[pltpu.VMEM((half, half), bf16)],
        compiler_params=pltpu.CompilerParams(vmem_limit_bytes=16 << 20),
        cost_estimate=pl.CostEstimate(flops=8 * half**3, bytes_accessed=20 * half**2, transcendentals=0),
        name="share",
    )(left, columns, right)


def complete_kernel(part, other, right, update, made, sems):
    size = part.shape[1]
    width = size // 4
    copies = []
    for index, low in enumerate(range(0, size, width)):
        columns = slice(low, low + width)
        product = jnp.dot(other[...], right[1, :, columns], preferred_element_type=f32)
        made[:, columns] = (part[:, columns].astype(f32) + product).astype(bf16)
        copies.append(
            pltpu.make_async_copy(made.at[:, columns], update.at[:, columns], sems.at[index])
        )
        copies[-1].start()
    for copy in copies:
        copy.wait()


def completed(part, other, right):
    half, size = part.shape
    return pl.pallas_call(
        complete_kernel,
        out_shape=jax.ShapeDtypeStruct((half, size), bf16),
        in_specs=[whole_in(pltpu.VMEM)] * 3,
        out_specs=whole_in(pl.ANY),
        scratch_shapes=[pltpu.VMEM((half, size), bf16), pltpu.SemaphoreType.DMA((4,))],
        compiler_params=pltpu.CompilerParams(vmem_limit_bytes=16 << 20),
        cost_estimate=pl.CostEstimate(flops=4 * half**3, bytes_accessed=16 * half**2, transcendentals=0),
        name="complete",
    )(part, other, right)


def statistics_kernel(core, own, other, stat, out, gradient):
    size = gradient.shape[0]
    tile = stat.shape[0]
    step = pl.program_id(0)
    mine = core[0]

    @pl.when((step == 0) & (mine == 0))
    def _():
        gradient[:, : size // 2] = own[...].reshape(size, size // 2)
        gradient[:, size // 2 :] = other[...].reshape(size, size // 2)

    @pl.when((step == 0) & (mine == 1))
    def _():
        gradient[:, size // 2 :] = own[...].reshape(size, size // 2)
        gradient[:, : size // 2] = other[...].reshape(size, size // 2)

    rows = pl.ds(pl.multiple_of(step * tile, tile), tile)

    @pl.when(mine == 0)
    def _():
        outer = lax.dot_general(
            gradient[rows, :], gradient[...], (((1,), (1,)), ((), ())), preferred_element_type=f32
        )
        out[...] = keep_rate * stat[...] + (1.0 - keep_rate) / size * outer

    @pl.when(mine == 1)
    def _():
        outer = lax.dot_general(
            gradient[:, rows], gradient[...], (((0,), (0,)), ((), ())), preferred_element_type=f32
        )
        out[...] = keep_rate * stat[...] + (1.0 - keep_rate) / size * outer


def statistics(core, own, other, stat):
    size = stat.shape[0]
    tile = size // 4
    block = pl.BlockSpec((tile, size), lambda step: (step, 0))
    return pl.pallas_call(
        statistics_kernel,
        grid=(size // tile,),
        out_shape=jax.ShapeDtypeStruct(stat.shape, f32),
        in_specs=[whole_in(pltpu.SMEM)] + [whole_in(pltpu.VMEM)] * 2 + [block],
        out_specs=block,
        scratch_shapes=[pltpu.VMEM((size, size), bf16)],
        compiler_params=pltpu.CompilerParams(vmem_limit_bytes=16 << 20),
        cost_estimate=pl.CostEstimate(flops=2 * size**3, bytes_accessed=12 * size**2, transcendentals=0),
        name="statistics",
    )(core, own, other, stat)


def step_kernel(places, old, update, low, high):
    half = low.shape[0]
    for block in range(2 * half):
        fresh = old[block].astype(f32) - step_size * update[places[block]].astype(f32)
        out = low if block < half else high
        out[block % half] = fresh.astype(bf16)


def stepped(places, old, update):
    shape = (old.shape[0] // 2,) + old.shape[1:]
    return pl.pallas_call(
        step_kernel,
        out_shape=[jax.ShapeDtypeStruct(shape, bf16)] * 2,
        in_specs=[whole_in(pltpu.SMEM)] + [whole_in(pltpu.VMEM)] * 2,
        out_specs=[whole_in(pltpu.VMEM)] * 2,
        compiler_params=pltpu.CompilerParams(vmem_limit_bytes=16 << 20),
        cost_estimate=pl.CostEstimate(flops=2 * old.size, bytes_accessed=6 * old.size, transcendentals=0),
        name="step",
    )(places, old, update)


def settle_kernel(replica, low_far, high_far, below, out, sems):
    half = low_far.shape[0]
    replicas = out.shape[0] // (2 * half)
    start = lax.rem(replica[0] + 2, replicas) * 2 * half
    copies = [
        pltpu.make_async_copy(piece, out.at[pl.ds(start + which * half, half)], sems.at[which])
        for which, piece in enumerate((low_far, high_far))
    ]
    for copy in copies:
        copy.start()
    for copy in copies:
        copy.wait()


def settled(replica, low_far, high_far, below):
    return pl.pallas_call(
        settle_kernel,
        out_shape=jax.ShapeDtypeStruct(below.shape, bf16),
        in_specs=[whole_in(pltpu.SMEM)] + [whole_in(pltpu.VMEM)] * 2 + [whole_in(pltpu.HBM)],
        out_specs=whole_in(pltpu.HBM),
        scratch_shapes=[pltpu.SemaphoreType.DMA((2,))],
        input_output_aliases={3: 0},
        compiler_params=pltpu.CompilerParams(vmem_limit_bytes=16 << 20),
        cost_estimate=pl.CostEstimate(flops=0, bytes_accessed=8 * low_far.size, transcendentals=0),
        name="settle",
    )(replica, low_far, high_far, below)


def on_device(grads, params, stats, roots, table):
    shards = lax.axis_size("shard")
    replicas = lax.axis_size("dp")
    blocks = grads.shape[1]
    group = blocks // replicas
    rows = grads.shape[2]
    size = grads.shape[3]
    half_rows = rows // 2
    half = group // 2
    replica = lax.axis_index("dp")
    core = (lax.axis_index("shard") % 2)[None]
    own_order = lax.dynamic_index_in_dim(table, replica, 0, keepdims=False)
    numbers = jnp.arange(group, dtype=table.dtype)
    own_places = jnp.max(
        jnp.where(own_order[None, :] == numbers[:, None], numbers[None, :], 0), axis=1
    )

    def piece(array, step, which):
        start = (replica + step) % replicas * group + which * half
        return lax.dynamic_slice_in_dim(array, start, half, 0)

    mine = grads[0]
    far = lax.optimization_barrier((piece(mine, 2, 0), piece(mine, 2, 1)))
    far_up = shifted(far[0], "dp", 1)
    far_down = shifted(far[1], "dp", -1)

    root = in_order((roots[0, 0],), far)[0]
    partner_root = other_core(root)
    mine = in_order((mine,), (partner_root,))[0]
    near = lax.optimization_barrier((piece(mine, 1, 1), piece(mine, 3, 0)))
    near_up = shifted(near[0], "dp", 1)
    near_down = shifted(near[1], "dp", -1)

    sums = lax.optimization_barrier(
        (added(piece(mine, 1, 0), far_up), added(piece(mine, 3, 1), far_down))
    )
    sum_up = shifted(sums[0], "dp", 1)
    sum_down = shifted(sums[1], "dp", -1)
    own, near_up, near_down = lax.optimization_barrier(
        (lax.dynamic_slice_in_dim(mine, replica * group, group, 0), near_up, near_down)
    )
    partial = lax.optimization_barrier((added(own[:half], near_down), added(own[half:], near_up)))
    root, partner_root = in_order((root, partner_root), partial)
    left, right = oriented(core, root, partner_root, half_rows)
    sum_up, sum_down, left, right = lax.optimization_barrier((sum_up, sum_down, left, right))
    whole = finish_sum(own_places, *partial, sum_up, sum_down)

    own_columns = exchanged(whole.reshape(shards, rows, size // 2))
    swapped = other_core(begun(left, own_columns))
    part = shared(left, own_columns, right)
    update = completed(part, swapped, right)

    own_columns = in_order((own_columns,), (update,))[0]
    update = exchanged(update.reshape(shards, half_rows, size))
    other_columns = other_core(own_columns)
    new_stat = statistics(core, own_columns, other_columns, stats[0, 0])
    own_params = lax.dynamic_slice_in_dim(params, replica * group, group, 0)
    update, new_stat, own_params = lax.optimization_barrier((update, new_stat, own_params))
    low, high = stepped(own_places, own_params, update.reshape(group, rows, size))
    low_below = shifted(low, "dp", 1)
    high_above = shifted(high, "dp", -1)
    high_below = shifted(high, "dp", 1)
    low_above = shifted(low, "dp", -1)
    low_far = shifted(low_below, "dp", 1)
    high_far = shifted(high_above, "dp", -1)

    def placed(out, block, step, which):
        start = (replica + step) % replicas * group + which * half
        return lax.dynamic_update_slice_in_dim(out, block, start, 0)

    out = jnp.zeros(params.shape, bf16)
    out = placed(out, low_below, 3, 0)
    out = placed(out, high_above, 1, 1)
    out = placed(out, low, 0, 0)
    out = placed(out, high, 0, 1)
    out = placed(out, high_below, 3, 1)
    out = placed(out, low_above, 1, 0)
    out = settled(replica[None], low_far, high_far, out)
    return (out, new_stat[None, None])


def solution(mesh):
    placed = (
        P("dp", None, "shard", None),
        P(None, "shard", None),
        P("dp", "shard", None, None),
        P("dp", "shard", None, None),
        P(),
    )
    return jax.shard_map(
        on_device,
        mesh=mesh,
        in_specs=placed,
        out_specs=(P(None, "shard", None), P("dp", "shard", None, None)),
        check_vma=False,
    )
```
